32 devices in a mesh: groups: 2 (over x), ex: 8 (over z, y), tp: 2 (over core).
Axes of the slice: x: 2, y: 2, z: 4, core: 2. Of those that a mesh axis runs over, the one named last changes fastest.
Arguments:
- activations: bfloat16 [16, 256, 29568], P(('groups', 'ex'), None, 'tp'), parts along dimension 0, may hold values from -6 to 6
- out_grads: bfloat16 [16, 256, 8192], P(('groups', 'ex'), None, 'tp'), parts along dimension 0, may hold values from -0.3984375 to 0.3984375
- in_factor: bfloat16 [32, 29568], P(None, 'tp'), may hold values from -0.03125 to 0.03125
- out_factor: bfloat16 [32, 8192], P(None, 'tp'), may hold values from -0.0625 to 0.0625
- curvature_inv: float32 [1024, 1024], P('tp'), may hold values from -1 to 4, as said below
- queries: bfloat16 [4096, 1024], P(('groups', 'ex'), 'tp'), parts along dimension 0, may hold values from -0.19921875 to 0.19921875
Outputs:
- example_grads: float32 [16, 1024], P(('groups', 'ex'), 'tp'), parts along dimension 0
- scores: float32 [16, 2048], P(('groups', 'ex'), 'tp'), parts along dimension 0
The draws below stay inside these ranges and needn't reach their ends.
There are 2 independent parts, one for each index of `groups`. The reference program is written for one: setup_inputs(seed, part) draws one part's arguments, and reference() takes and returns one part's arrays. A program takes and returns all parts, laid end to end along the dimension named above; an argument that names none is the same for every part. Nothing has to cross between parts.
Inputs may be any that keep to these rules, and one draw needn't show every extreme that they name: `curvature_inv`: symmetric.
All inputs are finite; a program needn't handle non-finite values.
Results may differ from the reference program's by a relative error of at most 0.0003.
Values may be sent and summed in bfloat16 or wider, within the bound.
No kernel may reach another device: no remote copies, remote signals or barrier semaphores. Data moves between devices by JAX's collectives and lax.ppermute only.
A program may use at most 128 MiB of HBM per device.

```python
import math
import jax
import jax.numpy as jnp
from jax import lax

FF = 29568
D = 8192
RANK = 32
TOK = 256
FEAT = 1024
EXAMPLES = 8
QUERIES = 2048


def draw_curvature_inv(key, part):
    key = jax.random.fold_in(key, 7)
    noise_key, diag_key = jax.random.split(key)
    noise = jax.random.normal(noise_key, (FEAT, FEAT), jnp.float32)
    symmetric = (noise + noise.T) * (0.35 / math.sqrt(2.0 * FEAT))
    diagonal = jax.random.uniform(diag_key, (FEAT,), jnp.float32, 1.0, 3.0)
    return symmetric + jnp.diag(diagonal)


def levels(own_key, shape, cuts, least, top_value):
    loudness = 1.0
    for dim, blocks in cuts:
        heights = jax.random.uniform(jax.random.fold_in(jax.random.fold_in(own_key, 6), dim), (blocks,), jnp.float32, least / len(cuts), top_value / len(cuts))
        loudness = loudness * jnp.repeat(jnp.exp(heights), shape[dim] // blocks).reshape((-1,) + (1,) * (len(shape) - 1 - dim))
    return loudness


def bell_draw(stream_key, extent, spread, reach, cuts=(), dtype=jnp.bfloat16):
    drawn = jax.random.normal(stream_key, extent, jnp.float32) * spread
    if len(cuts) > 0:
        drawn = levels(stream_key, extent, cuts, -0.22, 0.18) * drawn
    return jnp.clip(drawn, min=-reach, max=reach).astype(dtype)


def setup_inputs(seed: int = 0, part: int = 0) -> dict:
    arg_keys = jax.random.split(jax.random.key(seed), 7)
    part_keys = jax.random.split(jax.random.fold_in(arg_keys[6], part), 7)
    activations = bell_draw(part_keys[0], (EXAMPLES, TOK, FF), 1.0, 6.0, ((0, 8), (2, 2)))
    out_grads = bell_draw(part_keys[1], (EXAMPLES, TOK, D), 0.0625, 0.3984375, ((0, 8), (2, 2)))
    in_factor = bell_draw(arg_keys[2], (RANK, FF), FF ** -0.5, 0.03125, ((1, 2),))
    out_factor = bell_draw(arg_keys[3], (RANK, D), D ** -0.5, 0.0625, ((1, 2),))
    curvature_inv = draw_curvature_inv(jax.random.fold_in(arg_keys[6], 71), part)
    queries = bell_draw(part_keys[5], (QUERIES, FEAT), 0.03125, 0.19921875, ((0, 8), (1, 2)))
    return dict(activations=activations, out_grads=out_grads, in_factor=in_factor, out_factor=out_factor, curvature_inv=curvature_inv, queries=queries)


def reference(activations, out_grads, in_factor, out_factor, curvature_inv, queries):
    def per_example(pair):
        inputs, grads_row = pair
        in_proj = jnp.dot(inputs, in_factor.T, preferred_element_type=jnp.float32)
        out_proj = jnp.dot(grads_row, out_factor.T, preferred_element_type=jnp.float32)
        outer = jnp.dot(out_proj.T, in_proj, precision=lax.Precision.HIGHEST)
        return outer.reshape(-1)

    example_grads = lax.map(per_example, (activations, out_grads))
    precond = jnp.dot(example_grads, curvature_inv.T, precision=lax.Precision.HIGHEST)
    scores = jnp.dot(precond, queries.astype(jnp.float32).T, precision=lax.Precision.HIGHEST)
    return example_grads, scores
```

```python
import functools

import jax
import jax.numpy as jnp
from jax import lax
from jax.experimental import pallas as pl
from jax.experimental.pallas import tpu as pltpu
from jax.sharding import PartitionSpec as P

LANES = 128
CHUNK = 2048
NT = (((1,), (1,)), ((), ()))
ANY = pl.BlockSpec(memory_space=pl.ANY)
VMEM = pl.BlockSpec(memory_space=pltpu.VMEM)


def pieces(total, step):
    return [(start, min(step, total - start)) for start in range(0, total, step)]


def split(values, count):
    parts = []
    for _ in range(count):
        part = values.astype(jnp.bfloat16)
        parts.append(part)
        values = values - part.astype(jnp.float32)
    return parts


def project_kernel(acts, grads, in_f, out_f, result, acts_v, grads_v, in_v, out_v, sems):
    in_cuts = pieces(acts.shape[0], CHUNK)
    out_cuts = pieces(grads.shape[1], CHUNK)
    copies = [
        pltpu.make_async_copy(out_f, out_v, sems.at[0]),
        pltpu.make_async_copy(in_f, in_v, sems.at[1]),
    ]
    for start, size in out_cuts:
        cut = (slice(None), pl.ds(start, size))
        copies.append(pltpu.make_async_copy(grads.at[cut], grads_v.at[cut], sems.at[len(copies)]))
    for start, size in in_cuts:
        cut = pl.ds(start, size)
        copies.append(pltpu.make_async_copy(acts.at[cut], acts_v.at[cut], sems.at[len(copies)]))
    for copy in copies:
        copy.start()
    copies[0].wait()
    copies[1].wait()
    rank = in_f.shape[0]
    total = jnp.zeros((rank, grads.shape[0]), jnp.float32)
    for (start, size), copy in zip(out_cuts, copies[2:]):
        copy.wait()
        total += lax.dot_general(
            out_v[:, start : start + size],
            grads_v[:, start : start + size],
            NT,
            preferred_element_type=jnp.float32,
        )
    result[:rank] = total
    total = jnp.zeros_like(total)
    for (start, size), copy in zip(in_cuts, copies[2 + len(out_cuts) :]):
        copy.wait()
        total += jnp.dot(
            in_v[:, start : start + size],
            acts_v[start : start + size],
            preferred_element_type=jnp.float32,
        )
    result[rank:] = total


def project(acts, grads, in_factor, out_factor):
    shapes = (acts, grads, in_factor, out_factor)
    copies = 2 + len(pieces(acts.shape[0], CHUNK)) + len(pieces(grads.shape[1], CHUNK))
    rank, tokens = in_factor.shape[0], grads.shape[0]
    return pl.pallas_call(
        project_kernel,
        out_shape=jax.ShapeDtypeStruct((2 * rank, tokens), jnp.float32),
        in_specs=[ANY] * 4,
        out_specs=VMEM,
        scratch_shapes=[pltpu.VMEM(a.shape, a.dtype) for a in shapes]
        + [pltpu.SemaphoreType.DMA((copies,))],
        compiler_params=pltpu.CompilerParams(vmem_limit_bytes=32 << 20),
        cost_estimate=pl.CostEstimate(
            flops=2 * rank * tokens * (acts.shape[0] + grads.shape[1]),
            bytes_accessed=sum(a.size * 2 for a in shapes),
            transcendentals=0,
        ),
        name="project",
    )(*shapes)


def outer_kernel(mine, other, grad, share, lanes):
    rank = mine.shape[0] // 2
    for i in range(lanes.shape[0]):
        cut = slice(i * LANES, (i + 1) * LANES)
        lanes[i] = mine[:rank, cut] + other[:rank, cut]
    fold = LANES // rank
    rows = jnp.concatenate(
        [
            jnp.concatenate(
                [lanes[i, pl.ds(j, rank // fold, stride=fold), :] for j in range(fold)], axis=0
            )
            for i in range(lanes.shape[0])
        ],
        axis=1,
    )
    left = jnp.concatenate(split(rows, 3), axis=0)
    right = split(mine[rank:] + other[rank:], 3)
    wide = [jnp.concatenate([part] * fold, axis=0) for part in right]
    flat = jnp.zeros((rank, LANES), jnp.float32)
    for i, part in enumerate(wide):
        product = lax.dot_general(left, part, NT, preferred_element_type=jnp.float32)
        for j in range(3):
            flat += product[j * rank : (j + 1) * rank]
    column = lax.broadcasted_iota(jnp.int32, (rank // fold, LANES), 1) // rank
    result = jnp.zeros((rank // fold, LANES), jnp.float32)
    for j in range(fold):
        block = flat[j * (rank // fold) : (j + 1) * (rank // fold)]
        result += jnp.where(column == j, block, 0.0)
    grad[...] = result
    half = rank // fold // 2
    own = jnp.where(lax.axis_index("tp") == 0, result[:half], result[half:])
    for k in range(half):
        share[:, k * LANES : (k + 1) * LANES] = own[k : k + 1]


def outer(mine, other):
    rank, tokens = mine.shape[0] // 2, mine.shape[1]
    feats = rank * rank
    return pl.pallas_call(
        outer_kernel,
        out_shape=(
            jax.ShapeDtypeStruct((feats // LANES, LANES), jnp.float32),
            jax.ShapeDtypeStruct((1, feats // 2), jnp.float32),
        ),
        in_specs=[VMEM, VMEM],
        out_specs=(VMEM, VMEM),
        scratch_shapes=[pltpu.VMEM((tokens // LANES, rank, LANES), jnp.float32)],
        name="outer",
    )(mine, other)


def halves_kernel(values, high, low):
    whole = values[...]
    top = whole.astype(jnp.bfloat16)
    high[...] = top
    low[...] = (whole - top.astype(jnp.float32)).astype(jnp.bfloat16)


def halves(values):
    shape = jax.ShapeDtypeStruct(values.shape, jnp.bfloat16)
    return pl.pallas_call(
        halves_kernel,
        out_shape=(shape, shape),
        in_specs=[VMEM],
        out_specs=(VMEM, VMEM),
        cost_estimate=pl.CostEstimate(
            flops=3 * values.size, bytes_accessed=8 * values.size, transcendentals=0
        ),
        name="curvature_halves",
    )(values)


def score_kernel(blocks, near, far, high, low, *refs):
    queries, (kept, sent) = refs[:blocks], refs[blocks:]
    grads = jnp.concatenate(
        [
            jnp.concatenate([ref[k : k + 1] for k in range(ref.shape[0])], axis=1)
            for ref in (near, far)
        ],
        axis=0,
    )
    left = jnp.concatenate(split(grads, 3), axis=0)
    both = lax.dot_general(left, high[...], NT, preferred_element_type=jnp.float32)
    both += lax.dot_general(left, low[...], NT, preferred_element_type=jnp.float32)
    precond = both[0:2] + both[2:4] + both[4:6]
    left = jnp.concatenate(split(precond, 3), axis=0)
    place = lax.axis_index("ex") % blocks
    side = lax.axis_index("ex") // blocks
    keeps_near = lax.axis_index("tp") == side
    width = queries[0].shape[0]
    for j in range(blocks):
        triple = lax.dot_general(left, queries[j][...], NT, preferred_element_type=jnp.float32)
        total = triple[0:2] + triple[2:4] + triple[4:6]
        at = pl.ds(pl.multiple_of((place ^ j) * width, width), width)
        kept[:, at] = jnp.where(keeps_near, total[0:1], total[1:2])
        sent[:, at] = jnp.where(keeps_near, total[1:2], total[0:1])


def score(near, far, high, low, queries):
    row = jax.ShapeDtypeStruct((1, len(queries) * queries[0].shape[0]), jnp.float32)
    return pl.pallas_call(
        functools.partial(score_kernel, len(queries)),
        out_shape=(row, row),
        in_specs=[VMEM] * (4 + len(queries)),
        out_specs=(VMEM, VMEM),
        compiler_params=pltpu.CompilerParams(vmem_limit_bytes=32 << 20),
        name="score",
    )(near, far, high, low, *queries)


def shards(ex, activations, out_grads, in_factor, out_factor, curvature_inv, queries):
    half = ex // 2
    swap = [(0, 1), (1, 0)]
    crossing = [(i, i ^ (2 * half + 1)) for i in range(2 * ex)]
    blocks = [queries] + [
        lax.ppermute(queries, "ex", [(e, e ^ k) for e in range(ex)]) for k in range(1, half)
    ]
    part = project(activations[0].T, out_grads[0], in_factor, out_factor)
    grad, grads_share = outer(part, lax.ppermute(part, "tp", swap))
    far_grad = lax.ppermute(grad, ("ex", "tp"), crossing)
    high, low = halves(curvature_inv)
    kept, sent = score(grad, far_grad, high, low, blocks)
    summed = kept + lax.ppermute(sent, "tp", swap)
    returned = lax.ppermute(summed, ("ex", "tp"), crossing)
    keeps_near = lax.axis_index("tp") == lax.axis_index("ex") // half
    return grads_share, jnp.where(keeps_near, summed, returned)


def solution(mesh):
    placed = (
        P(("groups", "ex"), None, "tp"),
        P(("groups", "ex"), None, "tp"),
        P(None, "tp"),
        P(None, "tp"),
        P("tp", None),
        P(("groups", "ex"), "tp"),
    )
    return jax.shard_map(
        functools.partial(shards, mesh.shape["ex"]),
        mesh=mesh,
        in_specs=placed,
        out_specs=(P(("groups", "ex"), "tp"), P(("groups", "ex"), "tp")),
        check_vma=False,
    )
```

```python
import functools

import jax
import jax.numpy as jnp
from jax import lax
from jax.experimental import pallas as pl
from jax.experimental.pallas import tpu as pltpu
from jax.sharding import PartitionSpec as P

LANES = 128
CHUNK = 2048
NT = (((1,), (1,)), ((), ()))
ANY = pl.BlockSpec(memory_space=pl.ANY)
VMEM = pl.BlockSpec(memory_space=pltpu.VMEM)


def pieces(total, step):
    return [(start, min(step, total - start)) for start in range(0, total, step)]


def split(values, count):
    parts = []
    for _ in range(count):
        part = values.astype(jnp.bfloat16)
        parts.append(part)
        values = values - part.astype(jnp.float32)
    return parts


def project_kernel(token, acts, grads, in_f, out_f, result):
    rank = in_f.shape[0]
    result[:rank] = lax.dot_general(out_f[...], grads[...], NT, preferred_element_type=jnp.float32)
    result[rank:] = jnp.dot(in_f[...], acts[...], preferred_element_type=jnp.float32)


def project(token, acts, grads, in_factor, out_factor):
    shapes = (acts, grads, in_factor, out_factor)
    rank, tokens = in_factor.shape[0], grads.shape[0]
    return pl.pallas_call(
        project_kernel,
        out_shape=jax.ShapeDtypeStruct((2 * rank, tokens), jnp.float32),
        in_specs=[ANY] + [VMEM] * 4,
        out_specs=VMEM,
        compiler_params=pltpu.CompilerParams(vmem_limit_bytes=32 << 20),
        cost_estimate=pl.CostEstimate(
            flops=2 * rank * tokens * (acts.shape[0] + grads.shape[1]),
            bytes_accessed=sum(a.size * 2 for a in shapes),
            transcendentals=0,
        ),
        name="project",
    )(token, *shapes)


def outer_kernel(mine, other, grad, share, lanes):
    rank = mine.shape[0] // 2
    for i in range(lanes.shape[0]):
        cut = slice(i * LANES, (i + 1) * LANES)
        lanes[i] = mine[:rank, cut] + other[:rank, cut]
    fold = LANES // rank
    rows = jnp.concatenate(
        [
            jnp.concatenate(
                [lanes[i, pl.ds(j, rank // fold, stride=fold), :] for j in range(fold)], axis=0
            )
            for i in range(lanes.shape[0])
        ],
        axis=1,
    )
    left = jnp.concatenate(split(rows, 3), axis=0)
    right = split(mine[rank:] + other[rank:], 3)
    wide = [jnp.concatenate([part] * fold, axis=0) for part in right]
    flat = jnp.zeros((rank, LANES), jnp.float32)
    for i, part in enumerate(wide):
        product = lax.dot_general(left, part, NT, preferred_element_type=jnp.float32)
        for j in range(3):
            flat += product[j * rank : (j + 1) * rank]
    column = lax.broadcasted_iota(jnp.int32, (rank // fold, LANES), 1) // rank
    result = jnp.zeros((rank // fold, LANES), jnp.float32)
    for j in range(fold):
        block = flat[j * (rank // fold) : (j + 1) * (rank // fold)]
        result += jnp.where(column == j, block, 0.0)
    grad[...] = result
    half = rank // fold // 2
    own = jnp.where(lax.axis_index("tp") == 0, result[:half], result[half:])
    for k in range(half):
        share[:, k * LANES : (k + 1) * LANES] = own[k : k + 1]


def outer(mine, other):
    rank, tokens = mine.shape[0] // 2, mine.shape[1]
    feats = rank * rank
    return pl.pallas_call(
        outer_kernel,
        out_shape=(
            jax.ShapeDtypeStruct((feats // LANES, LANES), jnp.float32),
            jax.ShapeDtypeStruct((1, feats // 2), jnp.float32),
        ),
        in_specs=[VMEM, VMEM],
        out_specs=(VMEM, VMEM),
        scratch_shapes=[pltpu.VMEM((tokens // LANES, rank, LANES), jnp.float32)],
        compiler_params=pltpu.CompilerParams(vmem_limit_bytes=16 << 20),
        name="outer",
    )(mine, other)


def halves_kernel(values, queries, high, low, own, sem):
    copy = pltpu.make_async_copy(queries, own, sem)
    copy.start()
    whole = values[...]
    top = whole.astype(jnp.bfloat16)
    high[...] = top
    low[...] = (whole - top.astype(jnp.float32)).astype(jnp.bfloat16)
    copy.wait()


def halves(values, queries):
    shape = jax.ShapeDtypeStruct(values.shape, jnp.bfloat16)
    return pl.pallas_call(
        halves_kernel,
        out_shape=(shape, shape, jax.ShapeDtypeStruct(queries.shape, queries.dtype)),
        in_specs=[VMEM, ANY],
        out_specs=(VMEM, VMEM, VMEM),
        scratch_shapes=[pltpu.SemaphoreType.DMA(())],
        cost_estimate=pl.CostEstimate(
            flops=3 * values.size, bytes_accessed=8 * values.size, transcendentals=0
        ),
        compiler_params=pltpu.CompilerParams(vmem_limit_bytes=16 << 20),
        name="curvature_halves",
    )(values, queries)


def precond_kernel(near, far, high, low, parts):
    grads = jnp.concatenate(
        [
            jnp.concatenate([ref[k : k + 1] for k in range(ref.shape[0])], axis=1)
            for ref in (near, far)
        ],
        axis=0,
    )
    left = jnp.concatenate(split(grads, 3), axis=0)
    both = lax.dot_general(left, high[...], NT, preferred_element_type=jnp.float32)
    both += lax.dot_general(left, low[...], NT, preferred_element_type=jnp.float32)
    parts[...] = jnp.concatenate(split(both[0:2] + both[2:4] + both[4:6], 3), axis=0)


def precondition(near, far, high, low):
    return pl.pallas_call(
        precond_kernel,
        out_shape=jax.ShapeDtypeStruct((6, high.shape[0]), jnp.bfloat16),
        in_specs=[VMEM] * 4,
        out_specs=VMEM,
        compiler_params=pltpu.CompilerParams(vmem_limit_bytes=16 << 20),
        name="precondition",
    )(near, far, high, low)


def keeps_near(blocks):
    return lax.axis_index("tp") == lax.axis_index("ex") // blocks


def score_kernel(blocks, left, *refs):
    queries, (kept, sent) = refs[:blocks], refs[blocks:]
    place = lax.axis_index("ex") % blocks
    near = keeps_near(blocks)
    width = queries[0].shape[0]
    second = lax.axis_index("tp") == 1
    for j, steps in enumerate([(0, 0)] + gather_steps(blocks)):
        triple = lax.dot_general(
            left[...], queries[j][...], NT, preferred_element_type=jnp.float32
        )
        total = triple[0:2] + triple[2:4] + triple[4:6]
        at = pl.ds(pl.multiple_of((place ^ jnp.where(second, steps[1], steps[0])) * width, width), width)
        kept[:, at] = jnp.where(near, total[0:1], total[1:2])
        sent[:, at] = jnp.where(near, total[1:2], total[0:1])


def score(left, queries):
    row = jax.ShapeDtypeStruct((1, len(queries) * queries[0].shape[0]), jnp.float32)
    return pl.pallas_call(
        functools.partial(score_kernel, len(queries)),
        out_shape=(row, row),
        in_specs=[VMEM] * (1 + len(queries)),
        out_specs=(VMEM, VMEM),
        compiler_params=pltpu.CompilerParams(vmem_limit_bytes=16 << 20),
        name="score",
    )(left, *queries)


def finish_kernel(blocks, summed, returned, result):
    result[...] = jnp.where(keeps_near(blocks), summed[...], returned[...])


def finish(blocks, summed, returned):
    return pl.pallas_call(
        functools.partial(finish_kernel, blocks),
        out_shape=jax.ShapeDtypeStruct(summed.shape, summed.dtype),
        in_specs=[VMEM, VMEM],
        out_specs=VMEM,
        compiler_params=pltpu.CompilerParams(vmem_limit_bytes=16 << 20),
        name="finish",
    )(summed, returned)


def stage_kernel(values, result):
    result[...] = jnp.zeros_like(result)


def stage(values):
    return pl.pallas_call(
        stage_kernel,
        out_shape=jax.ShapeDtypeStruct((8, LANES), jnp.float32),
        in_specs=[ANY],
        out_specs=VMEM,
        compiler_params=pltpu.CompilerParams(vmem_limit_bytes=16 << 20),
        cost_estimate=pl.CostEstimate(flops=20_000_000_000, bytes_accessed=64 << 20, transcendentals=0),
        name="stage",
    )(values)


def gather_steps(half):
    other = {1: 2, 2: 1} if half > 2 else {}
    return [(k, other.get(k, k)) for k in range(1, half)]


def shards(ex, activations, out_grads, in_factor, out_factor, curvature_inv, queries):
    half = ex // 2
    swap = [(0, 1), (1, 0)]
    crossing = [(i, i ^ (2 * half + 1)) for i in range(2 * ex)]
    queries, token = lax.optimization_barrier((queries, stage(queries)))
    blocks = [queries]
    for steps in gather_steps(half):
        pairs = [(i, i ^ (2 * steps[i % 2])) for i in range(2 * ex)]
        blocks.append(lax.ppermute(queries, ("ex", "tp"), pairs))
    part = project(token, activations[0].T, out_grads[0], in_factor, out_factor)
    grad, grads_share = outer(part, lax.ppermute(part, "tp", swap))
    far_grad = lax.ppermute(grad, ("ex", "tp"), crossing)
    high, low, blocks[0] = halves(curvature_inv, queries)
    left = precondition(grad, far_grad, high, low)
    kept, sent = score(left, blocks)
    summed = kept + lax.ppermute(sent, "tp", swap)
    returned = lax.ppermute(summed, ("ex", "tp"), crossing)
    return grads_share, finish(half, summed, returned)


def solution(mesh):
    placed = (
        P(("groups", "ex"), None, "tp"),
        P(("groups", "ex"), None, "tp"),
        P(None, "tp"),
        P(None, "tp"),
        P("tp", None),
        P(("groups", "ex"), "tp"),
    )
    return jax.shard_map(
        functools.partial(shards, mesh.shape["ex"]),
        mesh=mesh,
        in_specs=placed,
        out_specs=(P(("groups", "ex"), "tp"), P(("groups", "ex"), "tp")),
        check_vma=False,
    )
```

```python
import functools

import jax
import jax.numpy as jnp
from jax import lax
from jax.experimental import pallas as pl
from jax.experimental.pallas import tpu as pltpu
from jax.sharding import PartitionSpec as P

LANES = 128
CHUNK = 2048
NT = (((1,), (1,)), ((), ()))
ANY = pl.BlockSpec(memory_space=pl.ANY)
VMEM = pl.BlockSpec(memory_space=pltpu.VMEM)


def pieces(total, step):
    return [(start, min(step, total - start)) for start in range(0, total, step)]


def split(values, count):
    parts = []
    for _ in range(count):
        part = values.astype(jnp.bfloat16)
        parts.append(part)
        values = values - part.astype(jnp.float32)
    return parts


def out_kernel(token, grads, out_f, result):
    result[...] = lax.dot_general(out_f[...], grads[...], NT, preferred_element_type=jnp.float32)


def in_kernel(out_part, acts, in_f, result):
    rank = in_f.shape[0]
    result[:rank] = out_part[...]
    result[rank:] = jnp.dot(in_f[...], acts[...], preferred_element_type=jnp.float32)


def project_out(token, grads, out_factor):
    return pl.pallas_call(
        out_kernel,
        out_shape=jax.ShapeDtypeStruct((out_factor.shape[0], grads.shape[0]), jnp.float32),
        in_specs=[ANY, VMEM, VMEM],
        out_specs=VMEM,
        compiler_params=pltpu.CompilerParams(vmem_limit_bytes=16 << 20),
        cost_estimate=pl.CostEstimate(
            flops=2 * out_factor.size * grads.shape[0],
            bytes_accessed=2 * (grads.size + out_factor.size),
            transcendentals=0,
        ),
        name="project_out",
    )(token, grads, out_factor)


def project_in(out_part, acts, in_factor):
    rank, tokens = out_part.shape
    return pl.pallas_call(
        in_kernel,
        out_shape=jax.ShapeDtypeStruct((2 * rank, tokens), jnp.float32),
        in_specs=[VMEM, VMEM, VMEM],
        out_specs=VMEM,
        compiler_params=pltpu.CompilerParams(vmem_limit_bytes=32 << 20),
        cost_estimate=pl.CostEstimate(
            flops=2 * in_factor.size * tokens,
            bytes_accessed=2 * (acts.size + in_factor.size),
            transcendentals=0,
        ),
        name="project_in",
    )(out_part, acts, in_factor)


def outer_kernel(mine, other, grad, lanes):
    rank = mine.shape[0] // 2
    for i in range(lanes.shape[0]):
        cut = slice(i * LANES, (i + 1) * LANES)
        lanes[i] = mine[:rank, cut] + other[:rank, cut]
    fold = LANES // rank
    rows = jnp.concatenate(
        [
            jnp.concatenate(
                [lanes[i, pl.ds(j, rank // fold, stride=fold), :] for j in range(fold)], axis=0
            )
            for i in range(lanes.shape[0])
        ],
        axis=1,
    )
    left = jnp.concatenate(split(rows, 3), axis=0)
    right = split(mine[rank:] + other[rank:], 3)
    wide = [jnp.concatenate([part] * fold, axis=0) for part in right]
    flat = jnp.zeros((rank, LANES), jnp.float32)
    for i, part in enumerate(wide):
        product = lax.dot_general(left, part, NT, preferred_element_type=jnp.float32)
        for j in range(3):
            flat += product[j * rank : (j + 1) * rank]
    column = lax.broadcasted_iota(jnp.int32, (rank // fold, LANES), 1) // rank
    result = jnp.zeros((rank // fold, LANES), jnp.float32)
    for j in range(fold):
        block = flat[j * (rank // fold) : (j + 1) * (rank // fold)]
        result += jnp.where(column == j, block, 0.0)
    grad[...] = result


def outer(mine, other):
    rank, tokens = mine.shape[0] // 2, mine.shape[1]
    return pl.pallas_call(
        outer_kernel,
        out_shape=jax.ShapeDtypeStruct((rank * rank // LANES, LANES), jnp.float32),
        in_specs=[VMEM, VMEM],
        out_specs=VMEM,
        scratch_shapes=[pltpu.VMEM((tokens // LANES, rank, LANES), jnp.float32)],
        compiler_params=pltpu.CompilerParams(vmem_limit_bytes=16 << 20),
        name="outer",
    )(mine, other)


def serves(half):
    return lax.axis_index("tp") == lax.axis_index("ex") // half


def small(name, kernel, out_shape, operands, in_hbm=(), scratch=()):
    specs = [ANY if i in in_hbm else VMEM for i in range(len(operands))]
    return pl.pallas_call(
        kernel,
        out_shape=out_shape,
        in_specs=specs,
        out_specs=jax.tree.map(lambda _: VMEM, out_shape),
        scratch_shapes=scratch,
        compiler_params=pltpu.CompilerParams(vmem_limit_bytes=16 << 20),
        cost_estimate=pl.CostEstimate(flops=1, bytes_accessed=1, transcendentals=0),
        name=name,
    )(*operands)


def prepare_kernel(queries, values, own, high, low, sem):
    copy = pltpu.make_async_copy(queries, own, sem)
    copy.start()
    whole = values[...]
    top = whole.astype(jnp.bfloat16)
    high[...] = top
    low[...] = (whole - top.astype(jnp.float32)).astype(jnp.bfloat16)
    copy.wait()


def prepare(queries, values):
    part = jax.ShapeDtypeStruct(values.shape, jnp.bfloat16)
    return small(
        "prepare",
        prepare_kernel,
        (jax.ShapeDtypeStruct(queries.shape, queries.dtype), part, part),
        (queries, values),
        in_hbm=(0,),
        scratch=[pltpu.SemaphoreType.DMA(())],
    )


def stack_kernel(*refs):
    *parts, result = refs
    for i, part in enumerate(parts):
        result[i] = part[...]


def stack(parts):
    shape = jax.ShapeDtypeStruct((len(parts), *parts[0].shape), parts[0].dtype)
    return small("stack", stack_kernel, shape, tuple(parts))


def precond_kernel(grad, high, low, result):
    row = jnp.concatenate([grad[k : k + 1] for k in range(grad.shape[0])], axis=1)
    left = jnp.concatenate(split(row, 3), axis=0)
    both = lax.dot_general(left, high[...], NT, preferred_element_type=jnp.float32)
    both += lax.dot_general(left, low[...], NT, preferred_element_type=jnp.float32)
    result[...] = both[0:1] + both[1:2] + both[2:3]


def precondition(grad, high, low):
    shape = jax.ShapeDtypeStruct((1, high.shape[0]), jnp.float32)
    return small("precondition", precond_kernel, shape, (grad, high, low))


def halves_kernel(mine, other, result):
    width = mine.shape[1]
    first = lax.axis_index("tp") == 0
    result[:, :width] = jnp.where(first, mine[...], other[...])
    result[:, width:] = jnp.where(first, other[...], mine[...])


def both_halves(mine, other):
    shape = jax.ShapeDtypeStruct((mine.shape[0], 2 * mine.shape[1]), mine.dtype)
    return small("both_halves", halves_kernel, shape, (mine, other))


def score_kernel(half, ways, last, *refs):
    rows, refs = ((), refs) if last else (refs[:2], refs[2:])
    mine, others, refs = refs[: len(ways)], refs[len(ways)], refs[len(ways) + 1 :]
    before, (near, far, *lefts) = (refs[:3], refs[3:]) if last else ((), refs)

    @pl.when(serves(half))
    def _():
        if last:
            near[...] = before[0][...]
            far[...] = before[1][...]
            left = before[2][...]
        else:
            values = jnp.concatenate([ref[...] for ref in rows], axis=0)
            left = jnp.concatenate(split(values, 3), axis=0)
            lefts[0][...] = left
        place = lax.axis_index("ex") % half
        second = lax.axis_index("tp") == 1
        feats = left.shape[1] // 2
        halves = [left[:, :feats], left[:, feats:]]
        halves = [jnp.where(second, halves[1 - i], halves[i]) for i in range(2)]
        for i, (first_way, second_way) in enumerate(ways):
            other = others[ways.index((second_way, first_way))] if len(others.shape) > 2 else others[...]
            sums = lax.dot_general(
                halves[0], mine[i][...], NT, preferred_element_type=jnp.float32
            ) + lax.dot_general(halves[1], other, NT, preferred_element_type=jnp.float32)
            total = sums[0:2] + sums[2:4] + sums[4:6]
            width = total.shape[1]
            start = (place ^ jnp.where(second, second_way, first_way)) * width
            at = pl.ds(pl.multiple_of(start, width), width)
            near[:, at] = total[0:1]
            far[:, at] = total[1:2]


def score(half, ways, rows, mine, others, before=()):
    row = jax.ShapeDtypeStruct((1, half * mine[0].shape[0]), jnp.float32)
    shapes = (row, row)
    if not before:
        shapes += (jax.ShapeDtypeStruct((3 * len(rows), rows[0].shape[1]), jnp.bfloat16),)
    return small(
        "score",
        functools.partial(score_kernel, half, tuple(ways), bool(before)),
        shapes,
        (*rows, *mine, others, *before),
    )


def finish_kernel(half, grad, near, returned, share, result):
    rows = grad.shape[0] // 2
    half_grad = jnp.where(lax.axis_index("tp") == 0, grad[:rows], grad[rows:])
    for k in range(rows):
        share[:, k * LANES : (k + 1) * LANES] = half_grad[k : k + 1]

    @pl.when(serves(half))
    def _():
        result[...] = near[...]

    @pl.when(jnp.logical_not(serves(half)))
    def _():
        result[...] = returned[...]


def finish(half, grad, near, returned):
    shapes = (
        jax.ShapeDtypeStruct((1, grad.size // 2), jnp.float32),
        jax.ShapeDtypeStruct(near.shape, near.dtype),
    )
    return small(
        "finish", functools.partial(finish_kernel, half), shapes, (grad, near, returned)
    )


def stage_kernel(values, result):
    result[...] = jnp.zeros_like(result)


def stage(values):
    return pl.pallas_call(
        stage_kernel,
        out_shape=jax.ShapeDtypeStruct((8, LANES), jnp.float32),
        in_specs=[ANY],
        out_specs=VMEM,
        compiler_params=pltpu.CompilerParams(vmem_limit_bytes=16 << 20),
        cost_estimate=pl.CostEstimate(flops=20_000_000_000, bytes_accessed=64 << 20, transcendentals=0),
        name="stage",
    )(values)


def shards(sizes, activations, out_grads, in_factor, out_factor, curvature_inv, queries):
    groups, ex = sizes
    half = ex // 2
    axes = ("groups", "ex", "tp")

    def send(values, target):
        number = lambda group, e, core: (group * ex + e) * 2 + core
        pairs = [
            (number(g, e, t), number(*target(g, e, t, t == e // half)))
            for g in range(groups)
            for e in range(ex)
            for t in range(2)
        ]
        return lax.ppermute(values, axes, pairs)

    def swap(values):
        return lax.ppermute(values, "tp", [(0, 1), (1, 0)])

    queries, token = lax.optimization_barrier((queries, stage(queries)))
    turn = {1: 2, 2: 1} if half > 3 else {}
    ways = [(turn.get(k, k), k) for k in range(1, half - 1)]
    early = [send(queries, lambda g, e, t, _: (g, e ^ way[t], t)) for way in ways]
    last = []
    if half > 1:
        far = half - 1
        aside = lambda g, e, t: ((g + 1) % groups, e, t) if groups > 1 else (g, e ^ far, t)
        last = [
            send(queries, lambda g, e, t, on: (g, e ^ far, t) if on else aside(g, e, t)),
            send(queries, lambda g, e, t, on: (g, e if on else e ^ far, 1 - t)),
        ]

    def whole(steps, *values):
        empty = lambda *_: jax.tree.map(lambda s: jnp.zeros(s.shape, s.dtype), shapes)
        shapes = jax.eval_shape(steps, *values)
        return lax.cond(lax.axis_index("ex") < ex, steps, empty, *values)

    def gradient(part, queries, values):
        own, high, low = prepare(queries, values)
        grad = outer(part, swap(part))
        half_precond = precondition(grad, high, low)
        return grad, both_halves(half_precond, swap(half_precond)), own

    def exchange(precond, *blocks):
        others = swap(stack(blocks))
        far = send(precond, lambda g, e, t, on: (g, e, 1 - t) if on else (g, e ^ half, t))
        return score(half, [(0, 0), *ways], (precond, far), blocks, others)

    part = project_in(project_out(token, out_grads[0], out_factor), activations[0].T, in_factor)
    grad, precond, own = gradient(part, queries, curvature_inv)
    precond, *blocks = lax.optimization_barrier((precond, own, *early))
    scores = whole(exchange, precond, *blocks)
    if last:
        way = half - 1
        scores = score(half, [(way, way)], (), last[:1], last[1], scores)
    near, far = scores[:2]
    returned = send(far, lambda g, e, t, on: (g, e ^ half, t) if on else (g, e, 1 - t))
    return finish(half, grad, near, returned)


def solution(mesh):
    placed = (
        P(("groups", "ex"), None, "tp"),
        P(("groups", "ex"), None, "tp"),
        P(None, "tp"),
        P(None, "tp"),
        P("tp", None),
        P(("groups", "ex"), "tp"),
    )
    return jax.shard_map(
        functools.partial(shards, (mesh.shape["groups"], mesh.shape["ex"])),
        mesh=mesh,
        in_specs=placed,
        out_specs=(P(("groups", "ex"), "tp"), P(("groups", "ex"), "tp")),
        check_vma=False,
    )
```

```python
import functools

import jax
import jax.numpy as jnp
from jax import lax
from jax.experimental import pallas as pl
from jax.experimental.pallas import tpu as pltpu
from jax.sharding import PartitionSpec as P

LANES = 128
CHUNK = 2048
NT = (((1,), (1,)), ((), ()))
ANY = pl.BlockSpec(memory_space=pl.ANY)
VMEM = pl.BlockSpec(memory_space=pltpu.VMEM)


def pieces(total, step):
    return [(start, min(step, total - start)) for start in range(0, total, step)]


def split(values, count):
    parts = []
    for _ in range(count):
        part = values.astype(jnp.bfloat16)
        parts.append(part)
        values = values - part.astype(jnp.float32)
    return parts


def out_kernel(token, grads, out_f, result):
    result[...] = lax.dot_general(out_f[...], grads[...], NT, preferred_element_type=jnp.float32)


def in_kernel(out_part, acts, in_f, queries, result, own, sem):
    copy = pltpu.make_async_copy(queries, own, sem)
    copy.start()
    rank = in_f.shape[0]
    result[:rank] = out_part[...]
    result[rank:] = jnp.dot(in_f[...], acts[...], preferred_element_type=jnp.float32)
    copy.wait()


def project_out(token, grads, out_factor):
    return pl.pallas_call(
        out_kernel,
        out_shape=jax.ShapeDtypeStruct((out_factor.shape[0], grads.shape[0]), jnp.float32),
        in_specs=[ANY, VMEM, VMEM],
        out_specs=VMEM,
        compiler_params=pltpu.CompilerParams(vmem_limit_bytes=16 << 20),
        cost_estimate=pl.CostEstimate(
            flops=2 * out_factor.size * grads.shape[0],
            bytes_accessed=2 * (grads.size + out_factor.size),
            transcendentals=0,
        ),
        name="project_out",
    )(token, grads, out_factor)


def project_in(out_part, acts, in_factor, queries):
    rank, tokens = out_part.shape
    return pl.pallas_call(
        in_kernel,
        out_shape=(
            jax.ShapeDtypeStruct((2 * rank, tokens), jnp.float32),
            jax.ShapeDtypeStruct(queries.shape, queries.dtype),
        ),
        in_specs=[VMEM, VMEM, VMEM, ANY],
        out_specs=(VMEM, VMEM),
        scratch_shapes=[pltpu.SemaphoreType.DMA(())],
        compiler_params=pltpu.CompilerParams(vmem_limit_bytes=32 << 20),
        cost_estimate=pl.CostEstimate(
            flops=2 * in_factor.size * tokens,
            bytes_accessed=2 * (acts.size + in_factor.size),
            transcendentals=0,
        ),
        name="project_in",
    )(out_part, acts, in_factor, queries)


def outer_kernel(mine, other, grad, lanes):
    rank = mine.shape[0] // 2
    for i in range(lanes.shape[0]):
        cut = slice(i * LANES, (i + 1) * LANES)
        lanes[i] = mine[:rank, cut] + other[:rank, cut]
    fold = LANES // rank
    rows = jnp.concatenate(
        [
            jnp.concatenate(
                [lanes[i, pl.ds(j, rank // fold, stride=fold), :] for j in range(fold)], axis=0
            )
            for i in range(lanes.shape[0])
        ],
        axis=1,
    )
    left = jnp.concatenate(split(rows, 3), axis=0)
    right = split(mine[rank:] + other[rank:], 3)
    wide = [jnp.concatenate([part] * fold, axis=0) for part in right]
    flat = jnp.zeros((rank, LANES), jnp.float32)
    for i, part in enumerate(wide):
        product = lax.dot_general(left, part, NT, preferred_element_type=jnp.float32)
        for j in range(3):
            flat += product[j * rank : (j + 1) * rank]
    column = lax.broadcasted_iota(jnp.int32, (rank // fold, LANES), 1) // rank
    result = jnp.zeros((rank // fold, LANES), jnp.float32)
    for j in range(fold):
        block = flat[j * (rank // fold) : (j + 1) * (rank // fold)]
        result += jnp.where(column == j, block, 0.0)
    grad[...] = result


def outer(mine, other):
    rank, tokens = mine.shape[0] // 2, mine.shape[1]
    return pl.pallas_call(
        outer_kernel,
        out_shape=jax.ShapeDtypeStruct((rank * rank // LANES, LANES), jnp.float32),
        in_specs=[VMEM, VMEM],
        out_specs=VMEM,
        scratch_shapes=[pltpu.VMEM((tokens // LANES, rank, LANES), jnp.float32)],
        compiler_params=pltpu.CompilerParams(vmem_limit_bytes=16 << 20),
        name="outer",
    )(mine, other)


def odd(place):
    return (place ^ (place // 2)) % 2


def serves(half):
    return lax.axis_index("tp") == lax.axis_index("ex") // half


def small(name, kernel, out_shape, operands, in_hbm=(), scratch=()):
    specs = [ANY if i in in_hbm else VMEM for i in range(len(operands))]
    return pl.pallas_call(
        kernel,
        out_shape=out_shape,
        in_specs=specs,
        out_specs=jax.tree.map(lambda _: VMEM, out_shape),
        scratch_shapes=scratch,
        compiler_params=pltpu.CompilerParams(vmem_limit_bytes=16 << 20),
        cost_estimate=pl.CostEstimate(flops=1, bytes_accessed=1, transcendentals=0),
        name=name,
    )(*operands)


def prepare_kernel(values, high, low):
    whole = values[...]
    top = whole.astype(jnp.bfloat16)
    high[...] = top
    low[...] = (whole - top.astype(jnp.float32)).astype(jnp.bfloat16)


def prepare(values):
    part = jax.ShapeDtypeStruct(values.shape, jnp.bfloat16)
    return small("prepare", prepare_kernel, (part, part), (values,))


def stack_kernel(*refs):
    *parts, result = refs
    for i, part in enumerate(parts):
        result[i] = part[...]


def stack(parts):
    shape = jax.ShapeDtypeStruct((len(parts), *parts[0].shape), parts[0].dtype)
    return small("stack", stack_kernel, shape, tuple(parts))


def precond_kernel(grad, high, low, result):
    row = jnp.concatenate([grad[k : k + 1] for k in range(grad.shape[0])], axis=1)
    left = jnp.concatenate(split(row, 3), axis=0)
    both = lax.dot_general(left, high[...], NT, preferred_element_type=jnp.float32)
    both += lax.dot_general(left, low[...], NT, preferred_element_type=jnp.float32)
    result[...] = both[0:1] + both[1:2] + both[2:3]


def precondition(grad, high, low):
    shape = jax.ShapeDtypeStruct((1, high.shape[0]), jnp.float32)
    return small("precondition", precond_kernel, shape, (grad, high, low))


def halves_kernel(mine, other, result):
    width = mine.shape[1]
    first = lax.axis_index("tp") == 0
    result[:, :width] = jnp.where(first, mine[...], other[...])
    result[:, width:] = jnp.where(first, other[...], mine[...])


def both_halves(mine, other):
    shape = jax.ShapeDtypeStruct((mine.shape[0], 2 * mine.shape[1]), mine.dtype)
    return small("both_halves", halves_kernel, shape, (mine, other))


def score_kernel(half, ways, last, *refs):
    rows, refs = ((), refs) if last else (refs[:2], refs[2:])
    mine, others, refs = refs[: len(ways)], refs[len(ways)], refs[len(ways) + 1 :]
    before, (near, far, *lefts) = (refs[:3], refs[3:]) if last else ((), refs)

    @pl.when(serves(half))
    def _():
        if last:
            near[...] = before[0][...]
            far[...] = before[1][...]
            left = before[2][...]
        else:
            values = jnp.concatenate([ref[...] for ref in rows], axis=0)
            left = jnp.concatenate(split(values, 3), axis=0)
            lefts[0][...] = left
        place = lax.axis_index("ex") % half
        second = lax.axis_index("tp") == 1
        feats = left.shape[1] // 2
        halves = [left[:, :feats], left[:, feats:]]
        halves = [jnp.where(second, halves[1 - i], halves[i]) for i in range(2)]
        for i, (first_way, second_way) in enumerate(ways):
            other = others[ways.index((second_way, first_way))] if len(others.shape) > 2 else others[...]
            sums = lax.dot_general(
                halves[0], mine[i][...], NT, preferred_element_type=jnp.float32
            ) + lax.dot_general(halves[1], other, NT, preferred_element_type=jnp.float32)
            total = sums[0:2] + sums[2:4] + sums[4:6]
            width = total.shape[1]
            swapped = second != (odd(place) == 1)
            start = (place ^ jnp.where(swapped, second_way, first_way)) * width
            at = pl.ds(pl.multiple_of(start, width), width)
            near[:, at] = total[0:1]
            far[:, at] = total[1:2]


def score(half, ways, rows, mine, others, before=()):
    row = jax.ShapeDtypeStruct((1, half * mine[0].shape[0]), jnp.float32)
    shapes = (row, row)
    if not before:
        shapes += (jax.ShapeDtypeStruct((3 * len(rows), rows[0].shape[1]), jnp.bfloat16),)
    return small(
        "score",
        functools.partial(score_kernel, half, tuple(ways), bool(before)),
        shapes,
        (*rows, *mine, others, *before),
    )


def finish_kernel(half, grad, near, returned, share, result):
    rows = grad.shape[0] // 2
    half_grad = jnp.where(lax.axis_index("tp") == 0, grad[:rows], grad[rows:])
    for k in range(rows):
        share[:, k * LANES : (k + 1) * LANES] = half_grad[k : k + 1]

    @pl.when(serves(half))
    def _():
        result[...] = near[...]

    @pl.when(jnp.logical_not(serves(half)))
    def _():
        result[...] = returned[...]


def finish(half, grad, near, returned):
    shapes = (
        jax.ShapeDtypeStruct((1, grad.size // 2), jnp.float32),
        jax.ShapeDtypeStruct(near.shape, near.dtype),
    )
    return small(
        "finish", functools.partial(finish_kernel, half), shapes, (grad, near, returned)
    )


def stage_kernel(values, result):
    result[...] = jnp.zeros_like(result)


def stage(values):
    return pl.pallas_call(
        stage_kernel,
        out_shape=jax.ShapeDtypeStruct((8, LANES), jnp.float32),
        in_specs=[ANY],
        out_specs=VMEM,
        compiler_params=pltpu.CompilerParams(vmem_limit_bytes=16 << 20),
        cost_estimate=pl.CostEstimate(flops=20_000_000_000, bytes_accessed=64 << 20, transcendentals=0),
        name="stage",
    )(values)


def shards(sizes, activations, out_grads, in_factor, out_factor, curvature_inv, queries):
    groups, ex = sizes
    half = ex // 2
    axes = ("groups", "ex", "tp")

    def send(values, target):
        number = lambda group, e, core: (group * ex + e) * 2 + core
        pairs = [
            (number(g, e, t), number(*target(g, e, t, t == e // half)))
            for g in range(groups)
            for e in range(ex)
            for t in range(2)
        ]
        return lax.ppermute(values, axes, pairs)

    def swap(values):
        return lax.ppermute(values, "tp", [(0, 1), (1, 0)])

    queries, token = lax.optimization_barrier((queries, stage(queries)))
    turn = {1: 2, 2: 1} if half > 3 else {}
    ways = [(turn.get(k, k), k) for k in range(1, half - 1)]
    early = [
        send(queries, lambda g, e, t, _: (g, e ^ way[1 - (t ^ odd(e))], t)) for way in ways
    ]
    last = []
    far = half - 1
    aside = lambda g, e, t: ((g + 1) % groups, e, t) if groups > 1 else (g, e ^ max(far, 1), t)
    if far:
        last = [
            send(queries, lambda g, e, t, on: (g, e ^ far, t) if on else aside(g, e, t)),
            send(queries, lambda g, e, t, on: (g, e if on else e ^ far, 1 - t)),
        ]

    def whole(steps, *values):
        empty = lambda *_: jax.tree.map(lambda s: jnp.zeros(s.shape, s.dtype), shapes)
        shapes = jax.eval_shape(steps, *values)
        return lax.cond(lax.axis_index("ex") < ex, steps, empty, *values)

    def gradient(part, high, low):
        grad = outer(part, swap(part))
        half_precond = precondition(grad, high, low)
        return grad, both_halves(half_precond, swap(half_precond))

    def forward(g, e, t, on):
        if e < half:
            return (g, e, 1 - t) if on else (g, e ^ half, t)
        return (g, e, 1 - t) if on else (g, e ^ half, t)

    def exchange(precond, *blocks):
        others = swap(stack(blocks))
        far = send(precond, forward)
        return score(half, [(0, 0), *ways], (precond, far), blocks, others)

    out_part = project_out(token, out_grads[0], out_factor)
    part, own = project_in(out_part, activations[0].T, in_factor, queries)
    high, low = prepare(curvature_inv)
    grad, precond = gradient(part, high, low)
    precond, *blocks = lax.optimization_barrier((precond, own, *early))
    scores = whole(exchange, precond, *blocks)
    if last:
        way = half - 1
        scores = score(half, [(way, way)], (), last[:1], last[1], scores)
    near, far = scores[:2]
    returned = send(far, lambda g, e, t, on: (g, e ^ half, t) if on else (g, e, 1 - t))
    return finish(half, grad, near, returned)


def solution(mesh):
    placed = (
        P(("groups", "ex"), None, "tp"),
        P(("groups", "ex"), None, "tp"),
        P(None, "tp"),
        P(None, "tp"),
        P("tp", None),
        P(("groups", "ex"), "tp"),
    )
    return jax.shard_map(
        functools.partial(shards, (mesh.shape["groups"], mesh.shape["ex"])),
        mesh=mesh,
        in_specs=placed,
        out_specs=(P(("groups", "ex"), "tp"), P(("groups", "ex"), "tp")),
        check_vma=False,
    )
```

```python
import functools

import jax
import jax.numpy as jnp
from jax import lax
from jax.experimental import pallas as pl
from jax.experimental.pallas import tpu as pltpu
from jax.sharding import PartitionSpec as P

LANES = 128
NT = (((1,), (1,)), ((), ()))
ANY = pl.BlockSpec(memory_space=pl.ANY)
VMEM = pl.BlockSpec(memory_space=pltpu.VMEM)


def split(values, count):
    parts = []
    for _ in range(count):
        part = values.astype(jnp.bfloat16)
        parts.append(part)
        values = values - part.astype(jnp.float32)
    return parts


def out_kernel(token, grads, out_f, result):
    result[...] = lax.dot_general(out_f[...], grads[...], NT, preferred_element_type=jnp.float32)


def in_kernel(out_part, acts, in_f, queries, result, own, sem):
    copy = pltpu.make_async_copy(queries, own, sem)
    copy.start()
    rank = in_f.shape[0]
    result[:rank] = out_part[...]
    result[rank:] = jnp.dot(in_f[...], acts[...], preferred_element_type=jnp.float32)
    copy.wait()


def project_out(token, grads, out_factor):
    return pl.pallas_call(
        out_kernel,
        out_shape=jax.ShapeDtypeStruct((out_factor.shape[0], grads.shape[0]), jnp.float32),
        in_specs=[ANY, VMEM, VMEM],
        out_specs=VMEM,
        compiler_params=pltpu.CompilerParams(vmem_limit_bytes=16 << 20),
        cost_estimate=pl.CostEstimate(
            flops=2 * out_factor.size * grads.shape[0],
            bytes_accessed=2 * (grads.size + out_factor.size),
            transcendentals=0,
        ),
        name="project_out",
    )(token, grads, out_factor)


def project_in(out_part, acts, in_factor, queries):
    rank, tokens = out_part.shape
    return pl.pallas_call(
        in_kernel,
        out_shape=(
            jax.ShapeDtypeStruct((2 * rank, tokens), jnp.float32),
            jax.ShapeDtypeStruct(queries.shape, queries.dtype),
        ),
        in_specs=[VMEM, VMEM, VMEM, ANY],
        out_specs=(VMEM, VMEM),
        scratch_shapes=[pltpu.SemaphoreType.DMA(())],
        compiler_params=pltpu.CompilerParams(vmem_limit_bytes=32 << 20),
        cost_estimate=pl.CostEstimate(
            flops=2 * in_factor.size * tokens,
            bytes_accessed=2 * (acts.size + in_factor.size),
            transcendentals=0,
        ),
        name="project_in",
    )(out_part, acts, in_factor, queries)


def outer_kernel(mine, other, grad, lanes):
    rank = mine.shape[0] // 2
    for i in range(lanes.shape[0]):
        cut = slice(i * LANES, (i + 1) * LANES)
        lanes[i] = mine[:rank, cut] + other[:rank, cut]
    fold = LANES // rank
    rows = jnp.concatenate(
        [
            jnp.concatenate(
                [lanes[i, pl.ds(j, rank // fold, stride=fold), :] for j in range(fold)], axis=0
            )
            for i in range(lanes.shape[0])
        ],
        axis=1,
    )
    left = jnp.concatenate(split(rows, 3), axis=0)
    right = split(mine[rank:] + other[rank:], 3)
    wide = [jnp.concatenate([part] * fold, axis=0) for part in right]
    flat = jnp.zeros((rank, LANES), jnp.float32)
    for i, part in enumerate(wide):
        product = lax.dot_general(left, part, NT, preferred_element_type=jnp.float32)
        for j in range(3):
            flat += product[j * rank : (j + 1) * rank]
    column = lax.broadcasted_iota(jnp.int32, (rank // fold, LANES), 1) // rank
    result = jnp.zeros((rank // fold, LANES), jnp.float32)
    for j in range(fold):
        block = flat[j * (rank // fold) : (j + 1) * (rank // fold)]
        result += jnp.where(column == j, block, 0.0)
    grad[...] = result


def outer(mine, other):
    rank, tokens = mine.shape[0] // 2, mine.shape[1]
    return pl.pallas_call(
        outer_kernel,
        out_shape=jax.ShapeDtypeStruct((rank * rank // LANES, LANES), jnp.float32),
        in_specs=[VMEM, VMEM],
        out_specs=VMEM,
        scratch_shapes=[pltpu.VMEM((tokens // LANES, rank, LANES), jnp.float32)],
        compiler_params=pltpu.CompilerParams(vmem_limit_bytes=16 << 20),
        name="outer",
    )(mine, other)


def odd(place):
    return (place ^ (place // 2)) % 2


def serves(half):
    return lax.axis_index("tp") == lax.axis_index("ex") // half


def small(name, kernel, out_shape, operands, in_hbm=(), scratch=()):
    specs = [ANY if i in in_hbm else VMEM for i in range(len(operands))]
    return pl.pallas_call(
        kernel,
        out_shape=out_shape,
        in_specs=specs,
        out_specs=jax.tree.map(lambda _: VMEM, out_shape),
        scratch_shapes=scratch,
        compiler_params=pltpu.CompilerParams(vmem_limit_bytes=16 << 20),
        cost_estimate=pl.CostEstimate(flops=1, bytes_accessed=1, transcendentals=0),
        name=name,
    )(*operands)


def prepare_kernel(values, high, low):
    whole = values[...]
    top = whole.astype(jnp.bfloat16)
    high[...] = top
    low[...] = (whole - top.astype(jnp.float32)).astype(jnp.bfloat16)


def prepare(values):
    part = jax.ShapeDtypeStruct(values.shape, jnp.bfloat16)
    return small("prepare", prepare_kernel, (part, part), (values,))


def keep_kernel(values, result):
    result[...] = values[...]


def keep(values):
    shape = jax.ShapeDtypeStruct(values.shape, values.dtype)
    return small("keep", keep_kernel, shape, (values,))


def stack_kernel(*refs):
    *parts, result = refs
    for i, part in enumerate(parts):
        result[i] = part[...]


def stack(parts):
    shape = jax.ShapeDtypeStruct((len(parts), *parts[0].shape), parts[0].dtype)
    return small("stack", stack_kernel, shape, tuple(parts))


def precond_kernel(grad, high, low, result):
    row = jnp.concatenate([grad[k : k + 1] for k in range(grad.shape[0])], axis=1)
    left = jnp.concatenate(split(row, 3), axis=0)
    both = lax.dot_general(left, high[...], NT, preferred_element_type=jnp.float32)
    both += lax.dot_general(left, low[...], NT, preferred_element_type=jnp.float32)
    result[...] = both[0:1] + both[1:2] + both[2:3]


def precondition(grad, high, low):
    shape = jax.ShapeDtypeStruct((1, high.shape[0]), jnp.float32)
    return small("precondition", precond_kernel, shape, (grad, high, low))


def halves_kernel(mine, other, result):
    width = mine.shape[1]
    first = lax.axis_index("tp") == 0
    result[:, :width] = jnp.where(first, mine[...], other[...])
    result[:, width:] = jnp.where(first, other[...], mine[...])


def both_halves(mine, other):
    shape = jax.ShapeDtypeStruct((mine.shape[0], 2 * mine.shape[1]), mine.dtype)
    return small("both_halves", halves_kernel, shape, (mine, other))


def score_kernel(half, ways, last, *refs):
    rows, refs = ((), refs) if last else (refs[:2], refs[2:])
    mine, others, refs = refs[: len(ways)], refs[len(ways)], refs[len(ways) + 1 :]
    before, (near, far, *lefts) = (refs[:3], refs[3:]) if last else ((), refs)

    @pl.when(serves(half))
    def _():
        if last:
            near[...] = before[0][...]
            far[...] = before[1][...]
            left = before[2][...]
        else:
            values = jnp.concatenate([ref[...] for ref in rows], axis=0)
            left = jnp.concatenate(split(values, 3), axis=0)
            lefts[0][...] = left
        place = lax.axis_index("ex") % half
        second = lax.axis_index("tp") == 1
        feats = left.shape[1] // 2
        halves = [left[:, :feats], left[:, feats:]]
        halves = [jnp.where(second, halves[1 - i], halves[i]) for i in range(2)]
        for i, (first_way, second_way) in enumerate(ways):
            other = others[ways.index((second_way, first_way))] if len(others.shape) > 2 else others[...]
            sums = lax.dot_general(
                halves[0], mine[i][...], NT, preferred_element_type=jnp.float32
            ) + lax.dot_general(halves[1], other, NT, preferred_element_type=jnp.float32)
            total = sums[0:2] + sums[2:4] + sums[4:6]
            width = total.shape[1]
            swapped = second != (odd(place) == 1)
            start = (place ^ jnp.where(swapped, second_way, first_way)) * width
            at = pl.ds(pl.multiple_of(start, width), width)
            near[:, at] = total[0:1]
            far[:, at] = total[1:2]


def score(half, ways, rows, mine, others, before=()):
    row = jax.ShapeDtypeStruct((1, half * mine[0].shape[0]), jnp.float32)
    shapes = (row, row)
    if not before:
        shapes += (jax.ShapeDtypeStruct((3 * len(rows), rows[0].shape[1]), jnp.bfloat16),)
    return small(
        "score",
        functools.partial(score_kernel, half, tuple(ways), bool(before)),
        shapes,
        (*rows, *mine, others, *before),
    )


def finish_kernel(half, grad, near, returned, share, result):
    rows = grad.shape[0] // 2
    half_grad = jnp.where(lax.axis_index("tp") == 0, grad[:rows], grad[rows:])
    for k in range(rows):
        share[:, k * LANES : (k + 1) * LANES] = half_grad[k : k + 1]

    @pl.when(serves(half))
    def _():
        result[...] = near[...]

    @pl.when(jnp.logical_not(serves(half)))
    def _():
        result[...] = returned[...]


def finish(half, grad, near, returned):
    shapes = (
        jax.ShapeDtypeStruct((1, grad.size // 2), jnp.float32),
        jax.ShapeDtypeStruct(near.shape, near.dtype),
    )
    return small(
        "finish", functools.partial(finish_kernel, half), shapes, (grad, near, returned)
    )


def stage_kernel(values, result):
    result[...] = jnp.zeros_like(result)


def stage(values):
    return pl.pallas_call(
        stage_kernel,
        out_shape=jax.ShapeDtypeStruct((8, LANES), jnp.float32),
        in_specs=[ANY],
        out_specs=VMEM,
        compiler_params=pltpu.CompilerParams(vmem_limit_bytes=16 << 20),
        cost_estimate=pl.CostEstimate(flops=20_000_000_000, bytes_accessed=64 << 20, transcendentals=0),
        name="stage",
    )(values)


def shards(sizes, activations, out_grads, in_factor, out_factor, curvature_inv, queries):
    groups, ex = sizes
    half = ex // 2
    axes = ("groups", "ex", "tp")

    def send(values, target):
        number = lambda group, e, core: (group * ex + e) * 2 + core
        pairs = [
            (number(g, e, t), number(*target(g, e, t, t == e // half)))
            for g in range(groups)
            for e in range(ex)
            for t in range(2)
        ]
        return lax.ppermute(values, axes, pairs)

    def swap(values):
        return lax.ppermute(values, "tp", [(0, 1), (1, 0)])

    queries, token = lax.optimization_barrier((queries, stage(queries)))
    turn = {1: 2, 2: 1} if half > 3 else {}
    ways = [(turn.get(k, k), k) for k in range(1, half - 1)]
    early = [
        send(queries, lambda g, e, t, _: (g, e ^ way[1 - (t ^ odd(e))], t)) for way in ways
    ]
    last = []
    far = half - 1
    aside = lambda g, e, t: ((g + 1) % groups, e, t) if groups > 1 else (g, e ^ max(far, 1), t)
    if far:
        last = [
            send(queries, lambda g, e, t, on: (g, e ^ far, t) if on else aside(g, e, t)),
            send(queries, lambda g, e, t, on: (g, e if on else e ^ far, 1 - t)),
        ]

    def whole(steps, *values):
        empty = lambda *_: jax.tree.map(lambda s: jnp.zeros(s.shape, s.dtype), shapes)
        shapes = jax.eval_shape(steps, *values)
        return lax.cond(lax.axis_index("ex") < ex, steps, empty, *values)

    def gradient(part, high, low):
        grad = outer(part, swap(part))
        half_precond = precondition(grad, high, low)
        return grad, both_halves(half_precond, swap(half_precond))

    def exchange(precond, *blocks):
        far = send(precond, lambda g, e, t, on: (g, e, 1 - t) if on else (g, e ^ half, t))
        others = whole(lambda *values: keep(swap(stack(values))), *blocks)
        return score(half, [(0, 0), *ways], (precond, far), blocks, others)

    out_part = project_out(token, out_grads[0], out_factor)
    part, own = project_in(out_part, activations[0].T, in_factor, queries)
    high, low = prepare(curvature_inv)
    grad, precond = gradient(part, high, low)
    precond, *blocks = lax.optimization_barrier((precond, own, *early))
    scores = whole(exchange, precond, *blocks)
    if last:
        way = half - 1
        scores = score(half, [(way, way)], (), last[:1], last[1], scores)
    near, far = scores[:2]
    returned = send(far, lambda g, e, t, on: (g, e ^ half, t) if on else (g, e, 1 - t))
    return finish(half, grad, near, returned)


def solution(mesh):
    placed = (
        P(("groups", "ex"), None, "tp"),
        P(("groups", "ex"), None, "tp"),
        P(None, "tp"),
        P(None, "tp"),
        P("tp", None),
        P(("groups", "ex"), "tp"),
    )
    return jax.shard_map(
        functools.partial(shards, (mesh.shape["groups"], mesh.shape["ex"])),
        mesh=mesh,
        in_specs=placed,
        out_specs=(P(("groups", "ex"), "tp"), P(("groups", "ex"), "tp")),
        check_vma=False,
    )
```

```python
import functools

import jax
import jax.numpy as jnp
from jax import lax
from jax.experimental import pallas as pl
from jax.experimental.pallas import tpu as pltpu
from jax.sharding import PartitionSpec as P

LANES = 128
NT = (((1,), (1,)), ((), ()))
ANY = pl.BlockSpec(memory_space=pl.ANY)
VMEM = pl.BlockSpec(memory_space=pltpu.VMEM)


def split(values, count):
    parts = []
    for _ in range(count):
        part = values.astype(jnp.bfloat16)
        parts.append(part)
        values = values - part.astype(jnp.float32)
    return parts


def out_kernel(token, grads, out_f, result):
    result[...] = lax.dot_general(out_f[...], grads[...], NT, preferred_element_type=jnp.float32)


def in_kernel(out_part, acts, in_f, queries, result, own, sem):
    copy = pltpu.make_async_copy(queries, own, sem)
    copy.start()
    rank = in_f.shape[0]
    result[:rank] = out_part[...]
    result[rank:] = jnp.dot(in_f[...], acts[...], preferred_element_type=jnp.float32)
    copy.wait()


def project_out(token, grads, out_factor):
    return pl.pallas_call(
        out_kernel,
        out_shape=jax.ShapeDtypeStruct((out_factor.shape[0], grads.shape[0]), jnp.float32),
        in_specs=[ANY, VMEM, VMEM],
        out_specs=VMEM,
        compiler_params=pltpu.CompilerParams(vmem_limit_bytes=16 << 20),
        cost_estimate=pl.CostEstimate(
            flops=2 * out_factor.size * grads.shape[0],
            bytes_accessed=2 * (grads.size + out_factor.size),
            transcendentals=0,
        ),
        name="project_out",
    )(token, grads, out_factor)


def project_in(out_part, acts, in_factor, queries):
    rank, tokens = out_part.shape
    return pl.pallas_call(
        in_kernel,
        out_shape=(
            jax.ShapeDtypeStruct((2 * rank, tokens), jnp.float32),
            jax.ShapeDtypeStruct(queries.shape, queries.dtype),
        ),
        in_specs=[VMEM, VMEM, VMEM, ANY],
        out_specs=(VMEM, VMEM),
        scratch_shapes=[pltpu.SemaphoreType.DMA(())],
        compiler_params=pltpu.CompilerParams(vmem_limit_bytes=32 << 20),
        cost_estimate=pl.CostEstimate(
            flops=2 * in_factor.size * tokens,
            bytes_accessed=2 * (acts.size + in_factor.size),
            transcendentals=0,
        ),
        name="project_in",
    )(out_part, acts, in_factor, queries)


def outer_kernel(mine, other, grad, lanes):
    rank = mine.shape[0] // 2
    for i in range(lanes.shape[0]):
        cut = slice(i * LANES, (i + 1) * LANES)
        lanes[i] = mine[:rank, cut] + other[:rank, cut]
    fold = LANES // rank
    rows = jnp.concatenate(
        [
            jnp.concatenate(
                [lanes[i, pl.ds(j, rank // fold, stride=fold), :] for j in range(fold)], axis=0
            )
            for i in range(lanes.shape[0])
        ],
        axis=1,
    )
    left = jnp.concatenate(split(rows, 3), axis=0)
    right = split(mine[rank:] + other[rank:], 3)
    wide = [jnp.concatenate([part] * fold, axis=0) for part in right]
    flat = jnp.zeros((rank, LANES), jnp.float32)
    for i, part in enumerate(wide):
        product = lax.dot_general(left, part, NT, preferred_element_type=jnp.float32)
        for j in range(3):
            flat += product[j * rank : (j + 1) * rank]
    column = lax.broadcasted_iota(jnp.int32, (rank // fold, LANES), 1) // rank
    result = jnp.zeros((rank // fold, LANES), jnp.float32)
    for j in range(fold):
        block = flat[j * (rank // fold) : (j + 1) * (rank // fold)]
        result += jnp.where(column == j, block, 0.0)
    grad[...] = result


def outer(mine, other):
    rank, tokens = mine.shape[0] // 2, mine.shape[1]
    return pl.pallas_call(
        outer_kernel,
        out_shape=jax.ShapeDtypeStruct((rank * rank // LANES, LANES), jnp.float32),
        in_specs=[VMEM, VMEM],
        out_specs=VMEM,
        scratch_shapes=[pltpu.VMEM((tokens // LANES, rank, LANES), jnp.float32)],
        compiler_params=pltpu.CompilerParams(vmem_limit_bytes=16 << 20),
        name="outer",
    )(mine, other)


def odd(place):
    return (place ^ (place // 2)) % 2


def serves(half):
    return lax.axis_index("tp") == lax.axis_index("ex") // half


def small(name, kernel, out_shape, operands, in_hbm=(), scratch=()):
    specs = [ANY if i in in_hbm else VMEM for i in range(len(operands))]
    return pl.pallas_call(
        kernel,
        out_shape=out_shape,
        in_specs=specs,
        out_specs=jax.tree.map(lambda _: VMEM, out_shape),
        scratch_shapes=scratch,
        compiler_params=pltpu.CompilerParams(vmem_limit_bytes=16 << 20),
        cost_estimate=pl.CostEstimate(flops=1, bytes_accessed=1, transcendentals=0),
        name=name,
    )(*operands)


def prepare_kernel(values, high, low):
    whole = values[...]
    top = whole.astype(jnp.bfloat16)
    high[...] = top
    low[...] = (whole - top.astype(jnp.float32)).astype(jnp.bfloat16)


def prepare(values):
    part = jax.ShapeDtypeStruct(values.shape, jnp.bfloat16)
    return small("prepare", prepare_kernel, (part, part), (values,))


def keep_kernel(values, result):
    result[...] = values[...]


def keep(values):
    shape = jax.ShapeDtypeStruct(values.shape, values.dtype)
    return small("keep", keep_kernel, shape, (values,))


def stack_kernel(*refs):
    *parts, result = refs
    for i, part in enumerate(parts):
        result[i] = part[...]


def stack(parts):
    shape = jax.ShapeDtypeStruct((len(parts), *parts[0].shape), parts[0].dtype)
    return small("stack", stack_kernel, shape, tuple(parts))


def precond_kernel(grad, high, low, result):
    row = jnp.concatenate([grad[k : k + 1] for k in range(grad.shape[0])], axis=1)
    left = jnp.concatenate(split(row, 3), axis=0)
    both = lax.dot_general(left, high[...], NT, preferred_element_type=jnp.float32)
    both += lax.dot_general(left, low[...], NT, preferred_element_type=jnp.float32)
    result[...] = both[0:1] + both[1:2] + both[2:3]


def precondition(grad, high, low):
    shape = jax.ShapeDtypeStruct((1, high.shape[0]), jnp.float32)
    return small("precondition", precond_kernel, shape, (grad, high, low))


def halves_kernel(mine, other, result):
    width = mine.shape[1]
    first = lax.axis_index("tp") == 0
    result[:, :width] = jnp.where(first, mine[...], other[...])
    result[:, width:] = jnp.where(first, other[...], mine[...])


def both_halves(mine, other):
    shape = jax.ShapeDtypeStruct((mine.shape[0], 2 * mine.shape[1]), mine.dtype)
    return small("both_halves", halves_kernel, shape, (mine, other))


def score_kernel(half, ways, last, *refs):
    rows, refs = ((), refs) if last else (refs[:2], refs[2:])
    mine, others, refs = refs[: len(ways)], refs[len(ways)], refs[len(ways) + 1 :]
    before, (near, far, *lefts) = (refs[:3], refs[3:]) if last else ((), refs)

    @pl.when(serves(half))
    def _():
        if last:
            near[...] = before[0][...]
            far[...] = before[1][...]
            left = before[2][...]
        else:
            values = jnp.concatenate([ref[...] for ref in rows], axis=0)
            left = jnp.concatenate(split(values, 3), axis=0)
            lefts[0][...] = left
        place = lax.axis_index("ex") % half
        second = lax.axis_index("tp") == 1
        feats = left.shape[1] // 2
        halves = [left[:, :feats], left[:, feats:]]
        halves = [jnp.where(second, halves[1 - i], halves[i]) for i in range(2)]
        for i, (first_way, second_way) in enumerate(ways):
            other = others[ways.index((second_way, first_way))] if len(others.shape) > 2 else others[...]
            sums = lax.dot_general(
                halves[0], mine[i][...], NT, preferred_element_type=jnp.float32
            ) + lax.dot_general(halves[1], other, NT, preferred_element_type=jnp.float32)
            total = sums[0:2] + sums[2:4] + sums[4:6]
            width = total.shape[1]
            swapped = second != (odd(place) == 1)
            start = (place ^ jnp.where(swapped, second_way, first_way)) * width
            at = pl.ds(pl.multiple_of(start, width), width)
            near[:, at] = total[0:1]
            far[:, at] = total[1:2]


def score(half, ways, rows, mine, others, before=()):
    row = jax.ShapeDtypeStruct((1, half * mine[0].shape[0]), jnp.float32)
    shapes = (row, row)
    if not before:
        shapes += (jax.ShapeDtypeStruct((3 * len(rows), rows[0].shape[1]), jnp.bfloat16),)
    return small(
        "score",
        functools.partial(score_kernel, half, tuple(ways), bool(before)),
        shapes,
        (*rows, *mine, others, *before),
    )


def finish_kernel(half, grad, near, returned, share, result):
    rows = grad.shape[0] // 2
    half_grad = jnp.where(lax.axis_index("tp") == 0, grad[:rows], grad[rows:])
    for k in range(rows):
        share[:, k * LANES : (k + 1) * LANES] = half_grad[k : k + 1]

    @pl.when(serves(half))
    def _():
        result[...] = near[...]

    @pl.when(jnp.logical_not(serves(half)))
    def _():
        result[...] = returned[...]


def finish(half, grad, near, returned):
    shapes = (
        jax.ShapeDtypeStruct((1, grad.size // 2), jnp.float32),
        jax.ShapeDtypeStruct(near.shape, near.dtype),
    )
    return small(
        "finish", functools.partial(finish_kernel, half), shapes, (grad, near, returned)
    )


def stage_kernel(values, result):
    result[...] = jnp.zeros_like(result)


def stage(values):
    return pl.pallas_call(
        stage_kernel,
        out_shape=jax.ShapeDtypeStruct((8, LANES), jnp.float32),
        in_specs=[ANY],
        out_specs=VMEM,
        compiler_params=pltpu.CompilerParams(vmem_limit_bytes=16 << 20),
        cost_estimate=pl.CostEstimate(flops=20_000_000_000, bytes_accessed=64 << 20, transcendentals=0),
        name="stage",
    )(values)


def shards(sizes, activations, out_grads, in_factor, out_factor, curvature_inv, queries):
    groups, ex = sizes
    half = ex // 2
    axes = ("groups", "ex", "tp")

    def send(values, target):
        number = lambda group, e, core: (group * ex + e) * 2 + core
        pairs = [
            (number(g, e, t), number(*target(g, e, t, t == e // half)))
            for g in range(groups)
            for e in range(ex)
            for t in range(2)
        ]
        return lax.ppermute(values, axes, pairs)

    def swap(values):
        return lax.ppermute(values, "tp", [(0, 1), (1, 0)])

    queries, token = lax.optimization_barrier((queries, stage(queries)))
    turn = {1: 2, 2: 1} if half > 3 else {}
    ways = [(turn.get(k, k), k) for k in range(1, half - 1)]
    early = [
        send(queries, lambda g, e, t, _: (g, e ^ way[1 - (t ^ odd(e))], t)) for way in ways
    ]
    last = []
    far = half - 1
    aside = lambda g, e, t: ((g + 1) % groups, e, t) if groups > 1 else (g, e ^ max(far, 1), t)
    if far:
        last = [
            send(queries, lambda g, e, t, on: (g, e ^ far, t) if on else aside(g, e, t)),
            send(queries, lambda g, e, t, on: (g, e if on else e ^ far, 1 - t)),
        ]

    def whole(steps, *values):
        empty = lambda *_: jax.tree.map(lambda s: jnp.zeros(s.shape, s.dtype), shapes)
        shapes = jax.eval_shape(steps, *values)
        return lax.cond(lax.axis_index("ex") < ex, steps, empty, *values)

    def gradient(part, high, low):
        grad = outer(part, swap(part))
        half_precond = precondition(grad, high, low)
        return grad, both_halves(half_precond, swap(half_precond))

    out_part = project_out(token, out_grads[0], out_factor)
    part, own = project_in(out_part, activations[0].T, in_factor, queries)
    high, low = prepare(curvature_inv)
    grad, precond = gradient(part, high, low)
    blocks = [own, *early]
    far_row = send(precond, lambda g, e, t, on: (g, e, 1 - t) if on else (g, e ^ half, t))
    others = whole(lambda *values: keep(swap(stack(values))), *blocks)
    scores = score(half, [(0, 0), *ways], (precond, far_row), blocks, others)
    if last:
        way = half - 1
        scores = score(half, [(way, way)], (), last[:1], last[1], scores)
    near, far = scores[:2]
    returned = send(far, lambda g, e, t, on: (g, e ^ half, t) if on else (g, e, 1 - t))
    return finish(half, grad, near, returned)


def solution(mesh):
    placed = (
        P(("groups", "ex"), None, "tp"),
        P(("groups", "ex"), None, "tp"),
        P(None, "tp"),
        P(None, "tp"),
        P("tp", None),
        P(("groups", "ex"), "tp"),
    )
    return jax.shard_map(
        functools.partial(shards, (mesh.shape["groups"], mesh.shape["ex"])),
        mesh=mesh,
        in_specs=placed,
        out_specs=(P(("groups", "ex"), "tp"), P(("groups", "ex"), "tp")),
        check_vma=False,
    )
```

```python
import functools

import jax
import jax.numpy as jnp
from jax import lax
from jax.experimental import pallas as pl
from jax.experimental.pallas import tpu as pltpu
from jax.sharding import PartitionSpec as P

LANES = 128
NT = (((1,), (1,)), ((), ()))
ANY = pl.BlockSpec(memory_space=pl.ANY)
VMEM = pl.BlockSpec(memory_space=pltpu.VMEM)


def split(values, count):
    parts = []
    for _ in range(count):
        part = values.astype(jnp.bfloat16)
        parts.append(part)
        values = values - part.astype(jnp.float32)
    return parts


def out_kernel(token, grads, out_f, result):
    result[...] = lax.dot_general(out_f[...], grads[...], NT, preferred_element_type=jnp.float32)


def in_kernel(out_part, acts, in_f, queries, result, own, sem):
    copy = pltpu.make_async_copy(queries, own, sem)
    copy.start()
    rank = in_f.shape[0]
    result[:rank] = out_part[...]
    result[rank:] = jnp.dot(in_f[...], acts[...], preferred_element_type=jnp.float32)
    copy.wait()


def project_out(token, grads, out_factor):
    return pl.pallas_call(
        out_kernel,
        out_shape=jax.ShapeDtypeStruct((out_factor.shape[0], grads.shape[0]), jnp.float32),
        in_specs=[ANY, VMEM, VMEM],
        out_specs=VMEM,
        compiler_params=pltpu.CompilerParams(vmem_limit_bytes=16 << 20),
        cost_estimate=pl.CostEstimate(
            flops=2 * out_factor.size * grads.shape[0],
            bytes_accessed=2 * (grads.size + out_factor.size),
            transcendentals=0,
        ),
        name="project_out",
    )(token, grads, out_factor)


def project_in(out_part, acts, in_factor, queries):
    rank, tokens = out_part.shape
    return pl.pallas_call(
        in_kernel,
        out_shape=(
            jax.ShapeDtypeStruct((2 * rank, tokens), jnp.float32),
            jax.ShapeDtypeStruct(queries.shape, queries.dtype),
        ),
        in_specs=[VMEM, VMEM, VMEM, ANY],
        out_specs=(VMEM, VMEM),
        scratch_shapes=[pltpu.SemaphoreType.DMA(())],
        compiler_params=pltpu.CompilerParams(vmem_limit_bytes=32 << 20),
        cost_estimate=pl.CostEstimate(
            flops=2 * in_factor.size * tokens,
            bytes_accessed=2 * (acts.size + in_factor.size),
            transcendentals=0,
        ),
        name="project_in",
    )(out_part, acts, in_factor, queries)


def outer_kernel(mine, other, grad, lanes):
    rank = mine.shape[0] // 2
    for i in range(lanes.shape[0]):
        cut = slice(i * LANES, (i + 1) * LANES)
        lanes[i, :rank] = mine[:rank, cut] + other[:rank, cut]
    fold = LANES // rank
    rows = jnp.concatenate(
        [
            jnp.concatenate(
                [lanes[i, pl.ds(j, rank // fold, stride=fold), :] for j in range(fold)], axis=0
            )
            for i in range(lanes.shape[0])
        ],
        axis=1,
    )
    left = jnp.concatenate(split(rows, 3), axis=0)
    right = split(mine[rank:] + other[rank:], 3)
    wide = [jnp.concatenate([part] * fold, axis=0) for part in right]
    flat = jnp.zeros((rank, LANES), jnp.float32)
    for i, part in enumerate(wide):
        product = lax.dot_general(left, part, NT, preferred_element_type=jnp.float32)
        for j in range(3):
            flat += product[j * rank : (j + 1) * rank]
    column = lax.broadcasted_iota(jnp.int32, (rank // fold, LANES), 1) // rank
    result = jnp.zeros((rank // fold, LANES), jnp.float32)
    for j in range(fold):
        block = flat[j * (rank // fold) : (j + 1) * (rank // fold)]
        result += jnp.where(column == j, block, 0.0)
    grad[...] = result


def outer(mine, other):
    rank, tokens = mine.shape[0] // 2, mine.shape[1]
    return pl.pallas_call(
        outer_kernel,
        out_shape=jax.ShapeDtypeStruct((rank * rank // LANES, LANES), jnp.float32),
        in_specs=[VMEM, VMEM],
        out_specs=VMEM,
        scratch_shapes=[pltpu.VMEM((tokens // LANES, rank + LANES // rank, LANES), jnp.float32)],
        compiler_params=pltpu.CompilerParams(vmem_limit_bytes=16 << 20),
        name="outer",
    )(mine, other)


def odd(place):
    return (place ^ (place // 2)) % 2


def serves(half):
    return lax.axis_index("tp") == lax.axis_index("ex") // half


def small(name, kernel, out_shape, operands, in_hbm=(), scratch=()):
    specs = [ANY if i in in_hbm else VMEM for i in range(len(operands))]
    return pl.pallas_call(
        kernel,
        out_shape=out_shape,
        in_specs=specs,
        out_specs=jax.tree.map(lambda _: VMEM, out_shape),
        scratch_shapes=scratch,
        compiler_params=pltpu.CompilerParams(vmem_limit_bytes=16 << 20),
        cost_estimate=pl.CostEstimate(flops=1, bytes_accessed=1, transcendentals=0),
        name=name,
    )(*operands)


def prepare_kernel(values, high, low):
    whole = values[...]
    top = whole.astype(jnp.bfloat16)
    high[...] = top
    low[...] = (whole - top.astype(jnp.float32)).astype(jnp.bfloat16)


def prepare(values):
    part = jax.ShapeDtypeStruct(values.shape, jnp.bfloat16)
    return small("prepare", prepare_kernel, (part, part), (values,))


def keep_kernel(values, result):
    result[...] = values[...]


def keep(values):
    shape = jax.ShapeDtypeStruct(values.shape, values.dtype)
    return small("keep", keep_kernel, shape, (values,))


def stack_kernel(*refs):
    *parts, result = refs
    for i, part in enumerate(parts):
        result[i] = part[...]


def stack(parts):
    shape = jax.ShapeDtypeStruct((len(parts), *parts[0].shape), parts[0].dtype)
    return small("stack", stack_kernel, shape, tuple(parts))


def precond_kernel(grad, high, low, result):
    row = jnp.concatenate([grad[k : k + 1] for k in range(grad.shape[0])], axis=1)
    left = jnp.concatenate(split(row, 3), axis=0)
    both = lax.dot_general(left, high[...], NT, preferred_element_type=jnp.float32)
    both += lax.dot_general(left, low[...], NT, preferred_element_type=jnp.float32)
    result[...] = both[0:1] + both[1:2] + both[2:3]


def precondition(grad, high, low):
    shape = jax.ShapeDtypeStruct((1, high.shape[0]), jnp.float32)
    return small("precondition", precond_kernel, shape, (grad, high, low))


def halves_kernel(mine, other, result):
    width = mine.shape[1]
    first = lax.axis_index("tp") == 0
    result[:, :width] = jnp.where(first, mine[...], other[...])
    result[:, width:] = jnp.where(first, other[...], mine[...])


def both_halves(mine, other):
    shape = jax.ShapeDtypeStruct((mine.shape[0], 2 * mine.shape[1]), mine.dtype)
    return small("both_halves", halves_kernel, shape, (mine, other))


def score_kernel(half, ways, last, *refs):
    rows, refs = ((), refs) if last else (refs[:2], refs[2:])
    mine, others, refs = refs[: len(ways)], refs[len(ways)], refs[len(ways) + 1 :]
    before, (near, far, *lefts) = (refs[:3], refs[3:]) if last else ((), refs)

    @pl.when(serves(half))
    def _():
        if last:
            near[...] = before[0][...]
            far[...] = before[1][...]
            left = before[2][...]
        else:
            values = jnp.concatenate([ref[...] for ref in rows], axis=0)
            left = jnp.concatenate(split(values, 3), axis=0)
            lefts[0][...] = left
        place = lax.axis_index("ex") % half
        second = lax.axis_index("tp") == 1
        feats = left.shape[1] // 2
        halves = [left[:, :feats], left[:, feats:]]
        halves = [jnp.where(second, halves[1 - i], halves[i]) for i in range(2)]
        for i, (first_way, second_way) in enumerate(ways):
            other = others[ways.index((second_way, first_way))] if len(others.shape) > 2 else others[...]
            sums = lax.dot_general(
                halves[0], mine[i][...], NT, preferred_element_type=jnp.float32
            ) + lax.dot_general(halves[1], other, NT, preferred_element_type=jnp.float32)
            total = sums[0:2] + sums[2:4] + sums[4:6]
            width = total.shape[1]
            swapped = second != (odd(place) == 1)
            start = (place ^ jnp.where(swapped, second_way, first_way)) * width
            at = pl.ds(pl.multiple_of(start, width), width)
            near[:, at] = total[0:1]
            far[:, at] = total[1:2]


def score(half, ways, rows, mine, others, before=()):
    row = jax.ShapeDtypeStruct((1, half * mine[0].shape[0]), jnp.float32)
    shapes = (row, row)
    if not before:
        shapes += (jax.ShapeDtypeStruct((3 * len(rows), rows[0].shape[1]), jnp.bfloat16),)
    return small(
        "score",
        functools.partial(score_kernel, half, tuple(ways), bool(before)),
        shapes,
        (*rows, *mine, others, *before),
    )


def finish_kernel(half, grad, near, returned, share, result):
    rows = grad.shape[0] // 2
    half_grad = jnp.where(lax.axis_index("tp") == 0, grad[:rows], grad[rows:])
    for k in range(rows):
        share[:, k * LANES : (k + 1) * LANES] = half_grad[k : k + 1]

    @pl.when(serves(half))
    def _():
        result[...] = near[...]

    @pl.when(jnp.logical_not(serves(half)))
    def _():
        result[...] = returned[...]


def finish(half, grad, near, returned):
    shapes = (
        jax.ShapeDtypeStruct((1, grad.size // 2), jnp.float32),
        jax.ShapeDtypeStruct(near.shape, near.dtype),
    )
    return small(
        "finish", functools.partial(finish_kernel, half), shapes, (grad, near, returned)
    )


def stage_kernel(values, result):
    result[...] = jnp.zeros_like(result)


def stage(values):
    return pl.pallas_call(
        stage_kernel,
        out_shape=jax.ShapeDtypeStruct((8, LANES), jnp.float32),
        in_specs=[ANY],
        out_specs=VMEM,
        compiler_params=pltpu.CompilerParams(vmem_limit_bytes=16 << 20),
        cost_estimate=pl.CostEstimate(flops=20_000_000_000, bytes_accessed=64 << 20, transcendentals=0),
        name="stage",
    )(values)


def shards(sizes, activations, out_grads, in_factor, out_factor, curvature_inv, queries):
    groups, ex = sizes
    half = ex // 2
    axes = ("groups", "ex", "tp")

    def send(values, target):
        number = lambda group, e, core: (group * ex + e) * 2 + core
        pairs = [
            (number(g, e, t), number(*target(g, e, t, t == e // half)))
            for g in range(groups)
            for e in range(ex)
            for t in range(2)
        ]
        return lax.ppermute(values, axes, pairs)

    def swap(values):
        return lax.ppermute(values, "tp", [(0, 1), (1, 0)])

    queries, token = lax.optimization_barrier((queries, stage(queries)))
    turn = {1: 2, 2: 1} if half > 3 else {}
    ways = [(turn.get(k, k), k) for k in range(1, half - 1)]
    early = [
        send(queries, lambda g, e, t, _: (g, e ^ way[1 - (t ^ odd(e))], t)) for way in ways
    ]
    last = []
    far = half - 1
    aside = lambda g, e, t: ((g + 1) % groups, e, t) if groups > 1 else (g, e ^ max(far, 1), t)
    if far:
        last = [
            send(queries, lambda g, e, t, on: (g, e ^ far, t) if on else aside(g, e, t)),
            send(queries, lambda g, e, t, on: (g, e if on else e ^ far, 1 - t)),
        ]

    def whole(steps, *values):
        empty = lambda *_: jax.tree.map(lambda s: jnp.zeros(s.shape, s.dtype), shapes)
        shapes = jax.eval_shape(steps, *values)
        return lax.cond(lax.axis_index("ex") < ex, steps, empty, *values)

    def gradient(part, high, low):
        grad = outer(part, swap(part))
        half_precond = precondition(grad, high, low)
        return grad, both_halves(half_precond, swap(half_precond))

    out_part = project_out(token, out_grads[0], out_factor)
    part, own = project_in(out_part, activations[0].T, in_factor, queries)
    high, low = prepare(curvature_inv)
    grad, precond = gradient(part, high, low)
    blocks = [own, *early]
    far_row = send(precond, lambda g, e, t, on: (g, e, 1 - t) if on else (g, e ^ half, t))
    others = whole(lambda *values: keep(swap(stack(values))), *blocks)
    scores = score(half, [(0, 0), *ways], (precond, far_row), blocks, others)
    if last:
        way = half - 1
        scores = score(half, [(way, way)], (), last[:1], last[1], scores)
    near, far = scores[:2]
    returned = send(far, lambda g, e, t, on: (g, e ^ half, t) if on else (g, e, 1 - t))
    return finish(half, grad, near, returned)


def solution(mesh):
    placed = (
        P(("groups", "ex"), None, "tp"),
        P(("groups", "ex"), None, "tp"),
        P(None, "tp"),
        P(None, "tp"),
        P("tp", None),
        P(("groups", "ex"), "tp"),
    )
    return jax.shard_map(
        functools.partial(shards, (mesh.shape["groups"], mesh.shape["ex"])),
        mesh=mesh,
        in_specs=placed,
        out_specs=(P(("groups", "ex"), "tp"), P(("groups", "ex"), "tp")),
        check_vma=False,
    )
```

```python
import functools

import jax
import jax.numpy as jnp
from jax import lax
from jax.experimental import pallas as pl
from jax.experimental.pallas import tpu as pltpu
from jax.sharding import PartitionSpec as P

LANES = 128
NT = (((1,), (1,)), ((), ()))
ANY = pl.BlockSpec(memory_space=pl.ANY)
VMEM = pl.BlockSpec(memory_space=pltpu.VMEM)


def split(values, count):
    parts = []
    for _ in range(count):
        part = values.astype(jnp.bfloat16)
        parts.append(part)
        values = values - part.astype(jnp.float32)
    return parts


def out_kernel(token, grads, out_f, result):
    for cut in range(0, grads.shape[0], LANES):
        columns = slice(cut, cut + LANES)
        result[:, columns] = lax.dot_general(
            out_f[...], grads[columns], NT, preferred_element_type=jnp.float32
        )


def in_kernel(out_part, acts, in_f, queries, result, own, sem):
    copy = pltpu.make_async_copy(queries, own, sem)
    copy.start()
    rank = in_f.shape[0]
    result[:rank] = out_part[...]
    for cut in range(0, acts.shape[1], LANES):
        columns = slice(cut, cut + LANES)
        result[rank:, columns] = jnp.dot(
            in_f[...], acts[:, columns], preferred_element_type=jnp.float32
        )
    copy.wait()


def project_out(token, grads, out_factor):
    return pl.pallas_call(
        out_kernel,
        out_shape=jax.ShapeDtypeStruct((out_factor.shape[0], grads.shape[0]), jnp.float32),
        in_specs=[ANY, VMEM, VMEM],
        out_specs=VMEM,
        compiler_params=pltpu.CompilerParams(vmem_limit_bytes=16 << 20),
        cost_estimate=pl.CostEstimate(
            flops=2 * out_factor.size * grads.shape[0],
            bytes_accessed=2 * (grads.size + out_factor.size),
            transcendentals=0,
        ),
        name="project_out",
    )(token, grads, out_factor)


def project_in(out_part, acts, in_factor, queries):
    rank, tokens = out_part.shape
    return pl.pallas_call(
        in_kernel,
        out_shape=(
            jax.ShapeDtypeStruct((2 * rank, tokens), jnp.float32),
            jax.ShapeDtypeStruct(queries.shape, queries.dtype),
        ),
        in_specs=[VMEM, VMEM, VMEM, ANY],
        out_specs=(VMEM, VMEM),
        scratch_shapes=[pltpu.SemaphoreType.DMA(())],
        compiler_params=pltpu.CompilerParams(vmem_limit_bytes=32 << 20),
        cost_estimate=pl.CostEstimate(
            flops=2 * in_factor.size * tokens,
            bytes_accessed=2 * (acts.size + in_factor.size),
            transcendentals=0,
        ),
        name="project_in",
    )(out_part, acts, in_factor, queries)


def outer_kernel(mine, other, grad, lanes):
    rank = mine.shape[0] // 2
    for i in range(lanes.shape[0]):
        cut = slice(i * LANES, (i + 1) * LANES)
        lanes[i, :rank] = mine[:rank, cut] + other[:rank, cut]
    fold = LANES // rank
    rows = jnp.concatenate(
        [
            jnp.concatenate(
                [lanes[i, pl.ds(j, rank // fold, stride=fold), :] for j in range(fold)], axis=0
            )
            for i in range(lanes.shape[0])
        ],
        axis=1,
    )
    left = jnp.concatenate(split(rows, 3), axis=0)
    right = split(mine[rank:] + other[rank:], 3)
    wide = [jnp.concatenate([part] * fold, axis=0) for part in right]
    flat = jnp.zeros((rank, LANES), jnp.float32)
    for i, part in enumerate(wide):
        product = lax.dot_general(left, part, NT, preferred_element_type=jnp.float32)
        for j in range(3):
            flat += product[j * rank : (j + 1) * rank]
    column = lax.broadcasted_iota(jnp.int32, (rank // fold, LANES), 1) // rank
    result = jnp.zeros((rank // fold, LANES), jnp.float32)
    for j in range(fold):
        block = flat[j * (rank // fold) : (j + 1) * (rank // fold)]
        result += jnp.where(column == j, block, 0.0)
    grad[...] = result


def outer(mine, other):
    rank, tokens = mine.shape[0] // 2, mine.shape[1]
    return pl.pallas_call(
        outer_kernel,
        out_shape=jax.ShapeDtypeStruct((rank * rank // LANES, LANES), jnp.float32),
        in_specs=[VMEM, VMEM],
        out_specs=VMEM,
        scratch_shapes=[pltpu.VMEM((tokens // LANES, rank + LANES // rank, LANES), jnp.float32)],
        compiler_params=pltpu.CompilerParams(vmem_limit_bytes=16 << 20),
        name="outer",
    )(mine, other)


def odd(place):
    return (place ^ (place // 2)) % 2


def serves(half):
    return lax.axis_index("tp") == lax.axis_index("ex") // half


def small(name, kernel, out_shape, operands, in_hbm=(), scratch=()):
    specs = [ANY if i in in_hbm else VMEM for i in range(len(operands))]
    return pl.pallas_call(
        kernel,
        out_shape=out_shape,
        in_specs=specs,
        out_specs=jax.tree.map(lambda _: VMEM, out_shape),
        scratch_shapes=scratch,
        compiler_params=pltpu.CompilerParams(vmem_limit_bytes=16 << 20),
        cost_estimate=pl.CostEstimate(flops=1, bytes_accessed=1, transcendentals=0),
        name=name,
    )(*operands)


def prepare_kernel(values, high, low):
    whole = values[...]
    top = whole.astype(jnp.bfloat16)
    high[...] = top
    low[...] = (whole - top.astype(jnp.float32)).astype(jnp.bfloat16)


def prepare(values):
    part = jax.ShapeDtypeStruct(values.shape, jnp.bfloat16)
    return small("prepare", prepare_kernel, (part, part), (values,))


def keep_kernel(values, result):
    result[...] = values[...]


def keep(values):
    shape = jax.ShapeDtypeStruct(values.shape, values.dtype)
    return small("keep", keep_kernel, shape, (values,))


def stack_kernel(*refs):
    *parts, result = refs
    for i, part in enumerate(parts):
        result[i] = part[...]


def stack(parts):
    shape = jax.ShapeDtypeStruct((len(parts), *parts[0].shape), parts[0].dtype)
    return small("stack", stack_kernel, shape, tuple(parts))


def precond_kernel(grad, high, low, result):
    row = jnp.concatenate([grad[k : k + 1] for k in range(grad.shape[0])], axis=1)
    left = jnp.concatenate(split(row, 3), axis=0)
    both = lax.dot_general(left, high[...], NT, preferred_element_type=jnp.float32)
    both += lax.dot_general(left, low[...], NT, preferred_element_type=jnp.float32)
    result[...] = both[0:1] + both[1:2] + both[2:3]


def precondition(grad, high, low):
    shape = jax.ShapeDtypeStruct((1, high.shape[0]), jnp.float32)
    return small("precondition", precond_kernel, shape, (grad, high, low))


def halves_kernel(mine, other, result):
    width = mine.shape[1]
    first = lax.axis_index("tp") == 0
    result[:, :width] = jnp.where(first, mine[...], other[...])
    result[:, width:] = jnp.where(first, other[...], mine[...])


def both_halves(mine, other):
    shape = jax.ShapeDtypeStruct((mine.shape[0], 2 * mine.shape[1]), mine.dtype)
    return small("both_halves", halves_kernel, shape, (mine, other))


def score_kernel(half, ways, last, *refs):
    rows, refs = ((), refs) if last else (refs[:2], refs[2:])
    mine, others, refs = refs[: len(ways)], refs[len(ways)], refs[len(ways) + 1 :]
    before, (near, far, *lefts) = (refs[:3], refs[3:]) if last else ((), refs)

    @pl.when(serves(half))
    def _():
        if last:
            near[...] = before[0][...]
            far[...] = before[1][...]
            left = before[2][...]
        else:
            values = jnp.concatenate([ref[...] for ref in rows], axis=0)
            left = jnp.concatenate(split(values, 3), axis=0)
            lefts[0][...] = left
        place = lax.axis_index("ex") % half
        second = lax.axis_index("tp") == 1
        feats = left.shape[1] // 2
        halves = [left[:, :feats], left[:, feats:]]
        halves = [jnp.where(second, halves[1 - i], halves[i]) for i in range(2)]
        for i, (first_way, second_way) in enumerate(ways):
            other = others[ways.index((second_way, first_way))] if len(others.shape) > 2 else others[...]
            sums = lax.dot_general(
                halves[0], mine[i][...], NT, preferred_element_type=jnp.float32
            ) + lax.dot_general(halves[1], other, NT, preferred_element_type=jnp.float32)
            total = sums[0:2] + sums[2:4] + sums[4:6]
            width = total.shape[1]
            swapped = second != (odd(place) == 1)
            start = (place ^ jnp.where(swapped, second_way, first_way)) * width
            at = pl.ds(pl.multiple_of(start, width), width)
            near[:, at] = total[0:1]
            far[:, at] = total[1:2]


def score(half, ways, rows, mine, others, before=()):
    row = jax.ShapeDtypeStruct((1, half * mine[0].shape[0]), jnp.float32)
    shapes = (row, row)
    if not before:
        shapes += (jax.ShapeDtypeStruct((3 * len(rows), rows[0].shape[1]), jnp.bfloat16),)
    return small(
        "score",
        functools.partial(score_kernel, half, tuple(ways), bool(before)),
        shapes,
        (*rows, *mine, others, *before),
    )


def finish_kernel(half, grad, near, returned, share, result):
    rows = grad.shape[0] // 2
    half_grad = jnp.where(lax.axis_index("tp") == 0, grad[:rows], grad[rows:])
    for k in range(rows):
        share[:, k * LANES : (k + 1) * LANES] = half_grad[k : k + 1]

    @pl.when(serves(half))
    def _():
        result[...] = near[...]

    @pl.when(jnp.logical_not(serves(half)))
    def _():
        result[...] = returned[...]


def finish(half, grad, near, returned):
    shapes = (
        jax.ShapeDtypeStruct((1, grad.size // 2), jnp.float32),
        jax.ShapeDtypeStruct(near.shape, near.dtype),
    )
    return small(
        "finish", functools.partial(finish_kernel, half), shapes, (grad, near, returned)
    )


def stage_kernel(values, result):
    result[...] = jnp.zeros_like(result)


def stage(values):
    return pl.pallas_call(
        stage_kernel,
        out_shape=jax.ShapeDtypeStruct((8, LANES), jnp.float32),
        in_specs=[ANY],
        out_specs=VMEM,
        compiler_params=pltpu.CompilerParams(vmem_limit_bytes=16 << 20),
        cost_estimate=pl.CostEstimate(flops=20_000_000_000, bytes_accessed=64 << 20, transcendentals=0),
        name="stage",
    )(values)


def shards(sizes, activations, out_grads, in_factor, out_factor, curvature_inv, queries):
    groups, ex = sizes
    half = ex // 2
    axes = ("groups", "ex", "tp")

    def send(values, target):
        number = lambda group, e, core: (group * ex + e) * 2 + core
        pairs = [
            (number(g, e, t), number(*target(g, e, t, t == e // half)))
            for g in range(groups)
            for e in range(ex)
            for t in range(2)
        ]
        return lax.ppermute(values, axes, pairs)

    def swap(values):
        return lax.ppermute(values, "tp", [(0, 1), (1, 0)])

    queries, token = lax.optimization_barrier((queries, stage(queries)))
    turn = {1: 2, 2: 1} if half > 3 else {}
    ways = [(turn.get(k, k), k) for k in range(1, half - 1)]
    early = [
        send(queries, lambda g, e, t, _: (g, e ^ way[1 - (t ^ odd(e))], t)) for way in ways
    ]
    last = []
    far = half - 1
    aside = lambda g, e, t: ((g + 1) % groups, e, t) if groups > 1 else (g, e ^ max(far, 1), t)
    if far:
        last = [
            send(queries, lambda g, e, t, on: (g, e ^ far, t) if on else aside(g, e, t)),
            send(queries, lambda g, e, t, on: (g, e if on else e ^ far, 1 - t)),
        ]

    def whole(steps, *values):
        empty = lambda *_: jax.tree.map(lambda s: jnp.zeros(s.shape, s.dtype), shapes)
        shapes = jax.eval_shape(steps, *values)
        return lax.cond(lax.axis_index("ex") < ex, steps, empty, *values)

    def gradient(part, high, low):
        grad = outer(part, swap(part))
        half_precond = precondition(grad, high, low)
        return grad, both_halves(half_precond, swap(half_precond))

    out_part = project_out(token, out_grads[0], out_factor)
    part, own = project_in(out_part, activations[0].T, in_factor, queries)
    high, low = prepare(curvature_inv)
    grad, precond = gradient(part, high, low)
    blocks = [own, *early]
    far_row = send(precond, lambda g, e, t, on: (g, e, 1 - t) if on else (g, e ^ half, t))
    others = whole(lambda *values: keep(swap(stack(values))), *blocks)
    scores = score(half, [(0, 0), *ways], (precond, far_row), blocks, others)
    if last:
        way = half - 1
        scores = score(half, [(way, way)], (), last[:1], last[1], scores)
    near, far = scores[:2]
    returned = send(far, lambda g, e, t, on: (g, e ^ half, t) if on else (g, e, 1 - t))
    return finish(half, grad, near, returned)


def solution(mesh):
    placed = (
        P(("groups", "ex"), None, "tp"),
        P(("groups", "ex"), None, "tp"),
        P(None, "tp"),
        P(None, "tp"),
        P("tp", None),
        P(("groups", "ex"), "tp"),
    )
    return jax.shard_map(
        functools.partial(shards, (mesh.shape["groups"], mesh.shape["ex"])),
        mesh=mesh,
        in_specs=placed,
        out_specs=(P(("groups", "ex"), "tp"), P(("groups", "ex"), "tp")),
        check_vma=False,
    )
```

```python
import functools

import jax
import jax.numpy as jnp
from jax import lax
from jax.experimental import pallas as pl
from jax.experimental.pallas import tpu as pltpu
from jax.sharding import PartitionSpec as P

LANES = 128
NT = (((1,), (1,)), ((), ()))
ANY = pl.BlockSpec(memory_space=pl.ANY)
VMEM = pl.BlockSpec(memory_space=pltpu.VMEM)


def split(values, count):
    parts = []
    for _ in range(count):
        part = values.astype(jnp.bfloat16)
        parts.append(part)
        values = values - part.astype(jnp.float32)
    return parts


def out_kernel(token, grads, out_f, result):
    result[...] = lax.dot_general(out_f[...], grads[...], NT, preferred_element_type=jnp.float32)


def in_kernel(out_part, acts, in_f, queries, result, own, sem):
    copy = pltpu.make_async_copy(queries, own, sem)
    copy.start()
    rank = in_f.shape[0]
    result[:rank] = out_part[...]
    result[rank:] = jnp.dot(in_f[...], acts[...], preferred_element_type=jnp.float32)
    copy.wait()


def project_out(token, grads, out_factor):
    return pl.pallas_call(
        out_kernel,
        out_shape=jax.ShapeDtypeStruct((out_factor.shape[0], grads.shape[0]), jnp.float32),
        in_specs=[ANY, VMEM, VMEM],
        out_specs=VMEM,
        compiler_params=pltpu.CompilerParams(vmem_limit_bytes=16 << 20),
        cost_estimate=pl.CostEstimate(
            flops=2 * out_factor.size * grads.shape[0],
            bytes_accessed=2 * (grads.size + out_factor.size),
            transcendentals=0,
        ),
        name="project_out",
    )(token, grads, out_factor)


def project_in(out_part, acts, in_factor, queries):
    rank, tokens = out_part.shape
    return pl.pallas_call(
        in_kernel,
        out_shape=(
            jax.ShapeDtypeStruct((2 * rank, tokens), jnp.float32),
            jax.ShapeDtypeStruct(queries.shape, queries.dtype),
        ),
        in_specs=[VMEM, VMEM, VMEM, ANY],
        out_specs=(VMEM, VMEM),
        scratch_shapes=[pltpu.SemaphoreType.DMA(())],
        compiler_params=pltpu.CompilerParams(vmem_limit_bytes=32 << 20),
        cost_estimate=pl.CostEstimate(
            flops=2 * in_factor.size * tokens,
            bytes_accessed=2 * (acts.size + in_factor.size),
            transcendentals=0,
        ),
        name="project_in",
    )(out_part, acts, in_factor, queries)


def outer_kernel(mine, other, grad, lanes):
    rank = mine.shape[0] // 2
    for i in range(lanes.shape[0]):
        cut = slice(i * LANES, (i + 1) * LANES)
        lanes[i, :rank] = mine[:rank, cut] + other[:rank, cut]
    fold = LANES // rank
    rows = jnp.concatenate(
        [
            jnp.concatenate(
                [lanes[i, pl.ds(j, rank // fold, stride=fold), :] for j in range(fold)], axis=0
            )
            for i in range(lanes.shape[0])
        ],
        axis=1,
    )
    left = jnp.concatenate(split(rows, 3), axis=0)
    right = split(mine[rank:] + other[rank:], 3)
    wide = [jnp.concatenate([part] * fold, axis=0) for part in right]
    flat = jnp.zeros((rank, LANES), jnp.float32)
    for i, part in enumerate(wide):
        product = lax.dot_general(left, part, NT, preferred_element_type=jnp.float32)
        for j in range(3):
            flat += product[j * rank : (j + 1) * rank]
    column = lax.broadcasted_iota(jnp.int32, (rank // fold, LANES), 1) // rank
    result = jnp.zeros((rank // fold, LANES), jnp.float32)
    for j in range(fold):
        block = flat[j * (rank // fold) : (j + 1) * (rank // fold)]
        result += jnp.where(column == j, block, 0.0)
    grad[...] = result


def outer(mine, other):
    rank, tokens = mine.shape[0] // 2, mine.shape[1]
    return pl.pallas_call(
        outer_kernel,
        out_shape=jax.ShapeDtypeStruct((rank * rank // LANES, LANES), jnp.float32),
        in_specs=[VMEM, VMEM],
        out_specs=VMEM,
        scratch_shapes=[pltpu.VMEM((tokens // LANES, rank + LANES // rank, LANES), jnp.float32)],
        compiler_params=pltpu.CompilerParams(vmem_limit_bytes=16 << 20),
        name="outer",
    )(mine, other)


def odd(place):
    return (place ^ (place // 2)) % 2


def serves(half):
    return lax.axis_index("tp") == lax.axis_index("ex") // half


def small(name, kernel, out_shape, operands, in_hbm=(), scratch=()):
    specs = [ANY if i in in_hbm else VMEM for i in range(len(operands))]
    return pl.pallas_call(
        kernel,
        out_shape=out_shape,
        in_specs=specs,
        out_specs=jax.tree.map(lambda _: VMEM, out_shape),
        scratch_shapes=scratch,
        compiler_params=pltpu.CompilerParams(vmem_limit_bytes=16 << 20),
        cost_estimate=pl.CostEstimate(flops=1, bytes_accessed=1, transcendentals=0),
        name=name,
    )(*operands)


def prepare_kernel(values, high, low):
    whole = values[...]
    top = whole.astype(jnp.bfloat16)
    high[...] = top
    low[...] = (whole - top.astype(jnp.float32)).astype(jnp.bfloat16)


def prepare(values):
    part = jax.ShapeDtypeStruct(values.shape, jnp.bfloat16)
    return small("prepare", prepare_kernel, (part, part), (values,))


def keep_kernel(values, result):
    result[...] = values[...]


def keep(values):
    shape = jax.ShapeDtypeStruct(values.shape, values.dtype)
    return small("keep", keep_kernel, shape, (values,))


def stack_kernel(*refs):
    *parts, result = refs
    for i, part in enumerate(parts):
        result[i] = part[...]


def stack(parts):
    shape = jax.ShapeDtypeStruct((len(parts), *parts[0].shape), parts[0].dtype)
    return small("stack", stack_kernel, shape, tuple(parts))


def precond_kernel(grad, high, low, result):
    row = jnp.concatenate([grad[k : k + 1] for k in range(grad.shape[0])], axis=1)
    left = jnp.concatenate(split(row, 3), axis=0)
    both = lax.dot_general(left, high[...], NT, preferred_element_type=jnp.float32)
    both += lax.dot_general(left, low[...], NT, preferred_element_type=jnp.float32)
    result[...] = both[0:1] + both[1:2] + both[2:3]


def precondition(grad, high, low):
    shape = jax.ShapeDtypeStruct((1, high.shape[0]), jnp.float32)
    return small("precondition", precond_kernel, shape, (grad, high, low))


def halves_kernel(mine, other, result):
    width = mine.shape[1]
    first = lax.axis_index("tp") == 0
    result[:, :width] = jnp.where(first, mine[...], other[...])
    result[:, width:] = jnp.where(first, other[...], mine[...])


def both_halves(mine, other):
    shape = jax.ShapeDtypeStruct((mine.shape[0], 2 * mine.shape[1]), mine.dtype)
    return small("both_halves", halves_kernel, shape, (mine, other))


def score_kernel(half, ways, *refs):
    rows, mine, others = refs[:2], refs[2 : 2 + len(ways)], refs[2 + len(ways)]
    near, far, mine_left, other_left = refs[3 + len(ways) :]

    @pl.when(serves(half))
    def _():
        values = jnp.concatenate([ref[...] for ref in rows], axis=0)
        left = jnp.concatenate(split(values, 3), axis=0)
        place = lax.axis_index("ex") % half
        second = lax.axis_index("tp") == 1
        feats = left.shape[1] // 2
        halves = [left[:, :feats], left[:, feats:]]
        halves = [jnp.where(second, halves[1 - i], halves[i]) for i in range(2)]
        mine_left[...], other_left[...] = halves
        for i, (first_way, second_way) in enumerate(ways):
            other = others[ways.index((second_way, first_way))]
            sums = lax.dot_general(
                halves[0], mine[i][...], NT, preferred_element_type=jnp.float32
            ) + lax.dot_general(halves[1], other, NT, preferred_element_type=jnp.float32)
            total = sums[0:2] + sums[2:4] + sums[4:6]
            width = total.shape[1]
            swapped = second != (odd(place) == 1)
            start = (place ^ jnp.where(swapped, second_way, first_way)) * width
            at = pl.ds(pl.multiple_of(start, width), width)
            near[:, at] = total[0:1]
            far[:, at] = total[1:2]


def score(half, ways, rows, mine, others):
    row = jax.ShapeDtypeStruct((1, half * mine[0].shape[0]), jnp.float32)
    left = jax.ShapeDtypeStruct((3 * len(rows), rows[0].shape[1] // 2), jnp.bfloat16)
    return small(
        "score",
        functools.partial(score_kernel, half, tuple(ways)),
        (row, row, left, left),
        (*rows, *mine, others),
    )


def last_kernel(half, mine, other, block, other_block, far_before, far, near_end):
    @pl.when(serves(half))
    def _():
        far[...] = far_before[...]
        sums = lax.dot_general(
            mine[...], block[...], NT, preferred_element_type=jnp.float32
        ) + lax.dot_general(other[...], other_block[...], NT, preferred_element_type=jnp.float32)
        total = sums[0:2] + sums[2:4] + sums[4:6]
        far[:, last_block(half, total.shape[1])] = total[1:2]
        near_end[...] = total[0:1]


def last_block(half, width):
    place = (lax.axis_index("ex") % half) ^ (half - 1)
    return pl.ds(pl.multiple_of(place * width, width), width)


def score_last(half, far, lefts, blocks):
    end = jax.ShapeDtypeStruct((1, blocks[0].shape[0]), jnp.float32)
    return small(
        "score_last",
        functools.partial(last_kernel, half),
        (jax.ShapeDtypeStruct(far.shape, jnp.float32), end),
        (*lefts, *blocks, far),
    )


def finish_kernel(half, grad, near, returned, *refs):
    near_end, (share, result) = refs[:-2], refs[-2:]
    rows = grad.shape[0] // 2
    half_grad = jnp.where(lax.axis_index("tp") == 0, grad[:rows], grad[rows:])
    for k in range(rows):
        share[:, k * LANES : (k + 1) * LANES] = half_grad[k : k + 1]

    @pl.when(serves(half))
    def _():
        result[...] = near[...]
        if near_end:
            result[:, last_block(half, near_end[0].shape[1])] = near_end[0][...]

    @pl.when(jnp.logical_not(serves(half)))
    def _():
        result[...] = returned[...]


def finish(half, grad, near, returned, near_end):
    shapes = (
        jax.ShapeDtypeStruct((1, grad.size // 2), jnp.float32),
        jax.ShapeDtypeStruct(near.shape, near.dtype),
    )
    return small(
        "finish", functools.partial(finish_kernel, half), shapes, (grad, near, returned, *near_end)
    )


def stage_kernel(values, result):
    result[...] = jnp.zeros_like(result)


def stage(values):
    return pl.pallas_call(
        stage_kernel,
        out_shape=jax.ShapeDtypeStruct((8, LANES), jnp.float32),
        in_specs=[ANY],
        out_specs=VMEM,
        compiler_params=pltpu.CompilerParams(vmem_limit_bytes=16 << 20),
        cost_estimate=pl.CostEstimate(flops=20_000_000_000, bytes_accessed=64 << 20, transcendentals=0),
        name="stage",
    )(values)


def shards(sizes, activations, out_grads, in_factor, out_factor, curvature_inv, queries):
    groups, ex = sizes
    half = ex // 2
    axes = ("groups", "ex", "tp")

    def send(values, target):
        number = lambda group, e, core: (group * ex + e) * 2 + core
        pairs = [
            (number(g, e, t), number(*target(g, e, t, t == e // half)))
            for g in range(groups)
            for e in range(ex)
            for t in range(2)
        ]
        return lax.ppermute(values, axes, pairs)

    def swap(values):
        return lax.ppermute(values, "tp", [(0, 1), (1, 0)])

    queries, token = lax.optimization_barrier((queries, stage(queries)))
    turn = {1: 2, 2: 1} if half > 3 else {}
    ways = [(turn.get(k, k), k) for k in range(1, half - 1)]
    early = [
        send(queries, lambda g, e, t, _: (g, e ^ way[1 - (t ^ odd(e))], t)) for way in ways
    ]
    last = []
    far = half - 1
    aside = lambda g, e, t: ((g + 1) % groups, e, t) if groups > 1 else (g, e ^ max(far, 1), t)
    if far:
        last = [
            send(queries, lambda g, e, t, on: (g, e ^ far, t) if on else aside(g, e, t)),
            send(queries, lambda g, e, t, on: (g, e if on else e ^ far, 1 - t)),
        ]

    def whole(steps, *values):
        empty = lambda *_: jax.tree.map(lambda s: jnp.zeros(s.shape, s.dtype), shapes)
        shapes = jax.eval_shape(steps, *values)
        return lax.cond(lax.axis_index("ex") < ex, steps, empty, *values)

    def gradient(part, high, low):
        grad = outer(part, swap(part))
        half_precond = precondition(grad, high, low)
        return grad, both_halves(half_precond, swap(half_precond))

    out_part = project_out(token, out_grads[0], out_factor)
    part, own = project_in(out_part, activations[0].T, in_factor, queries)
    high, low = prepare(curvature_inv)
    grad, precond = gradient(part, high, low)
    blocks = [own, *early]
    far_row = send(precond, lambda g, e, t, on: (g, e, 1 - t) if on else (g, e ^ half, t))
    others = whole(lambda *values: keep(swap(stack(values))), *blocks)
    near, far_scores, *lefts = score(half, [(0, 0), *ways], (precond, far_row), blocks, others)
    near_end = []
    if last:
        far_scores, *near_end = score_last(half, far_scores, lefts, last)
    returned = send(far_scores, lambda g, e, t, on: (g, e ^ half, t) if on else (g, e, 1 - t))
    return finish(half, grad, near, returned, near_end)


def solution(mesh):
    placed = (
        P(("groups", "ex"), None, "tp"),
        P(("groups", "ex"), None, "tp"),
        P(None, "tp"),
        P(None, "tp"),
        P("tp", None),
        P(("groups", "ex"), "tp"),
    )
    return jax.shard_map(
        functools.partial(shards, (mesh.shape["groups"], mesh.shape["ex"])),
        mesh=mesh,
        in_specs=placed,
        out_specs=(P(("groups", "ex"), "tp"), P(("groups", "ex"), "tp")),
        check_vma=False,
    )
```

```python
import functools

import jax
import jax.numpy as jnp
from jax import lax
from jax.experimental import pallas as pl
from jax.experimental.pallas import tpu as pltpu
from jax.sharding import PartitionSpec as P

LANES = 128
NT = (((1,), (1,)), ((), ()))
ANY = pl.BlockSpec(memory_space=pl.ANY)
VMEM = pl.BlockSpec(memory_space=pltpu.VMEM)


def split(values, count):
    parts = []
    for _ in range(count):
        part = values.astype(jnp.bfloat16)
        parts.append(part)
        values = values - part.astype(jnp.float32)
    return parts


def out_kernel(token, grads, out_f, result):
    result[...] = lax.dot_general(out_f[...], grads[...], NT, preferred_element_type=jnp.float32)


def in_kernel(out_part, acts, in_f, queries, result, own, sem):
    copy = pltpu.make_async_copy(queries, own, sem)
    copy.start()
    rank = in_f.shape[0]
    result[:rank] = out_part[...]
    result[rank:] = jnp.dot(in_f[...], acts[...], preferred_element_type=jnp.float32)
    copy.wait()


def project_out(token, grads, out_factor):
    return pl.pallas_call(
        out_kernel,
        out_shape=jax.ShapeDtypeStruct((out_factor.shape[0], grads.shape[0]), jnp.float32),
        in_specs=[ANY, VMEM, VMEM],
        out_specs=VMEM,
        compiler_params=pltpu.CompilerParams(vmem_limit_bytes=16 << 20),
        cost_estimate=pl.CostEstimate(
            flops=2 * out_factor.size * grads.shape[0],
            bytes_accessed=2 * (grads.size + out_factor.size),
            transcendentals=0,
        ),
        name="project_out",
    )(token, grads, out_factor)


def project_in(out_part, acts, in_factor, queries):
    rank, tokens = out_part.shape
    return pl.pallas_call(
        in_kernel,
        out_shape=(
            jax.ShapeDtypeStruct((2 * rank, tokens), jnp.float32),
            jax.ShapeDtypeStruct(queries.shape, queries.dtype),
        ),
        in_specs=[VMEM, VMEM, VMEM, ANY],
        out_specs=(VMEM, VMEM),
        scratch_shapes=[pltpu.SemaphoreType.DMA(())],
        compiler_params=pltpu.CompilerParams(vmem_limit_bytes=32 << 20),
        cost_estimate=pl.CostEstimate(
            flops=2 * in_factor.size * tokens,
            bytes_accessed=2 * (acts.size + in_factor.size),
            transcendentals=0,
        ),
        name="project_in",
    )(out_part, acts, in_factor, queries)


def outer_kernel(mine, other, grad, lanes):
    rank = mine.shape[0] // 2
    for i in range(lanes.shape[0]):
        cut = slice(i * LANES, (i + 1) * LANES)
        lanes[i, :rank] = mine[:rank, cut] + other[:rank, cut]
    fold = LANES // rank
    rows = jnp.concatenate(
        [
            jnp.concatenate(
                [lanes[i, pl.ds(j, rank // fold, stride=fold), :] for j in range(fold)], axis=0
            )
            for i in range(lanes.shape[0])
        ],
        axis=1,
    )
    left = jnp.concatenate(split(rows, 3), axis=0)
    right = split(mine[rank:] + other[rank:], 3)
    wide = [jnp.concatenate([part] * fold, axis=0) for part in right]
    flat = jnp.zeros((rank, LANES), jnp.float32)
    for i, part in enumerate(wide):
        product = lax.dot_general(left, part, NT, preferred_element_type=jnp.float32)
        for j in range(3):
            flat += product[j * rank : (j + 1) * rank]
    column = lax.broadcasted_iota(jnp.int32, (rank // fold, LANES), 1) // rank
    result = jnp.zeros((rank // fold, LANES), jnp.float32)
    for j in range(fold):
        block = flat[j * (rank // fold) : (j + 1) * (rank // fold)]
        result += jnp.where(column == j, block, 0.0)
    grad[...] = result


def outer(mine, other):
    rank, tokens = mine.shape[0] // 2, mine.shape[1]
    return pl.pallas_call(
        outer_kernel,
        out_shape=jax.ShapeDtypeStruct((rank * rank // LANES, LANES), jnp.float32),
        in_specs=[VMEM, VMEM],
        out_specs=VMEM,
        scratch_shapes=[pltpu.VMEM((tokens // LANES, rank + LANES // rank, LANES), jnp.float32)],
        compiler_params=pltpu.CompilerParams(vmem_limit_bytes=16 << 20),
        name="outer",
    )(mine, other)


def odd(place):
    return (place ^ (place // 2)) % 2


def serves(half):
    return lax.axis_index("tp") == lax.axis_index("ex") // half


def small(name, kernel, out_shape, operands, in_hbm=(), scratch=()):
    specs = [ANY if i in in_hbm else VMEM for i in range(len(operands))]
    return pl.pallas_call(
        kernel,
        out_shape=out_shape,
        in_specs=specs,
        out_specs=jax.tree.map(lambda _: VMEM, out_shape),
        scratch_shapes=scratch,
        compiler_params=pltpu.CompilerParams(vmem_limit_bytes=16 << 20),
        cost_estimate=pl.CostEstimate(flops=1, bytes_accessed=1, transcendentals=0),
        name=name,
    )(*operands)


def prepare_kernel(values, high, low):
    whole = values[...]
    top = whole.astype(jnp.bfloat16)
    high[...] = top
    low[...] = (whole - top.astype(jnp.float32)).astype(jnp.bfloat16)


def prepare(values):
    part = jax.ShapeDtypeStruct(values.shape, jnp.bfloat16)
    return small("prepare", prepare_kernel, (part, part), (values,))


def keep_kernel(values, result):
    result[...] = values[...]


def keep(values):
    shape = jax.ShapeDtypeStruct(values.shape, values.dtype)
    return small("keep", keep_kernel, shape, (values,))


def stack_kernel(*refs):
    *parts, result = refs
    for i, part in enumerate(parts):
        result[i] = part[...]


def stack(parts):
    shape = jax.ShapeDtypeStruct((len(parts), *parts[0].shape), parts[0].dtype)
    return small("stack", stack_kernel, shape, tuple(parts))


def precond_kernel(grad, high, low, result):
    row = jnp.concatenate([grad[k : k + 1] for k in range(grad.shape[0])], axis=1)
    left = jnp.concatenate(split(row, 3), axis=0)
    both = lax.dot_general(left, high[...], NT, preferred_element_type=jnp.float32)
    both += lax.dot_general(left, low[...], NT, preferred_element_type=jnp.float32)
    result[...] = both[0:1] + both[1:2] + both[2:3]


def precondition(grad, high, low):
    shape = jax.ShapeDtypeStruct((1, high.shape[0]), jnp.float32)
    return small("precondition", precond_kernel, shape, (grad, high, low))


def halves_kernel(mine, other, result):
    width = mine.shape[1]
    first = lax.axis_index("tp") == 0
    result[:, :width] = jnp.where(first, mine[...], other[...])
    result[:, width:] = jnp.where(first, other[...], mine[...])


def both_halves(mine, other):
    shape = jax.ShapeDtypeStruct((mine.shape[0], 2 * mine.shape[1]), mine.dtype)
    return small("both_halves", halves_kernel, shape, (mine, other))


def score_kernel(half, ways, last, *refs):
    rows, refs = ((), refs) if last else (refs[:2], refs[2:])
    mine, others, refs = refs[: len(ways)], refs[len(ways)], refs[len(ways) + 1 :]
    before, (near, far, *lefts) = (refs[:3], refs[3:]) if last else ((), refs)

    @pl.when(serves(half))
    def _():
        if last:
            near[...] = before[0][...]
            far[...] = before[1][...]
            left = before[2][...]
        else:
            values = jnp.concatenate([ref[...] for ref in rows], axis=0)
            left = jnp.concatenate(split(values, 3), axis=0)
            lefts[0][...] = left
        place = lax.axis_index("ex") % half
        second = lax.axis_index("tp") == 1
        feats = left.shape[1] // 2
        halves = [left[:, :feats], left[:, feats:]]
        halves = [jnp.where(second, halves[1 - i], halves[i]) for i in range(2)]
        for i, (first_way, second_way) in enumerate(ways):
            other = others[ways.index((second_way, first_way))] if len(others.shape) > 2 else others[...]
            sums = lax.dot_general(
                halves[0], mine[i][...], NT, preferred_element_type=jnp.float32
            ) + lax.dot_general(halves[1], other, NT, preferred_element_type=jnp.float32)
            total = sums[0:2] + sums[2:4] + sums[4:6]
            width = total.shape[1]
            swapped = second != (odd(place) == 1)
            start = (place ^ jnp.where(swapped, second_way, first_way)) * width
            at = pl.ds(pl.multiple_of(start, width), width)
            near[:, at] = total[0:1]
            far[:, at] = total[1:2]


def score(half, ways, rows, mine, others, before=()):
    row = jax.ShapeDtypeStruct((1, half * mine[0].shape[0]), jnp.float32)
    shapes = (row, row)
    if not before:
        shapes += (jax.ShapeDtypeStruct((3 * len(rows), rows[0].shape[1]), jnp.bfloat16),)
    return small(
        "score",
        functools.partial(score_kernel, half, tuple(ways), bool(before)),
        shapes,
        (*rows, *mine, others, *before),
    )


def finish_kernel(half, grad, near, returned, share, result, row, sems):
    on = serves(half)
    kept = pltpu.make_async_copy(near, result, sems.at[0])
    got = pltpu.make_async_copy(returned, result, sems.at[0])
    pl.when(on)(kept.start)
    pl.when(jnp.logical_not(on))(got.start)
    rows = grad.shape[0] // 2
    half_grad = jnp.where(lax.axis_index("tp") == 0, grad[:rows], grad[rows:])
    for k in range(rows):
        row[:, k * LANES : (k + 1) * LANES] = half_grad[k : k + 1]
    written = pltpu.make_async_copy(row, share, sems.at[1])
    written.start()
    written.wait()
    pl.when(on)(kept.wait)
    pl.when(jnp.logical_not(on))(got.wait)


def finish(half, grad, near, returned):
    share = jax.ShapeDtypeStruct((1, grad.size // 2), jnp.float32)
    return pl.pallas_call(
        functools.partial(finish_kernel, half),
        out_shape=(share, jax.ShapeDtypeStruct(near.shape, near.dtype)),
        in_specs=[VMEM] * 3,
        out_specs=(ANY, ANY),
        scratch_shapes=[pltpu.VMEM(share.shape, share.dtype), pltpu.SemaphoreType.DMA((2,))],
        compiler_params=pltpu.CompilerParams(vmem_limit_bytes=16 << 20),
        cost_estimate=pl.CostEstimate(flops=1, bytes_accessed=1, transcendentals=0),
        name="finish",
    )(grad, near, returned)


def stage_kernel(values, result):
    result[...] = jnp.zeros_like(result)


def stage(values):
    return pl.pallas_call(
        stage_kernel,
        out_shape=jax.ShapeDtypeStruct((8, LANES), jnp.float32),
        in_specs=[ANY],
        out_specs=VMEM,
        compiler_params=pltpu.CompilerParams(vmem_limit_bytes=16 << 20),
        cost_estimate=pl.CostEstimate(flops=20_000_000_000, bytes_accessed=64 << 20, transcendentals=0),
        name="stage",
    )(values)


def shards(sizes, activations, out_grads, in_factor, out_factor, curvature_inv, queries):
    groups, ex = sizes
    half = ex // 2
    axes = ("groups", "ex", "tp")

    def send(values, target):
        number = lambda group, e, core: (group * ex + e) * 2 + core
        pairs = [
            (number(g, e, t), number(*target(g, e, t, t == e // half)))
            for g in range(groups)
            for e in range(ex)
            for t in range(2)
        ]
        return lax.ppermute(values, axes, pairs)

    def swap(values):
        return lax.ppermute(values, "tp", [(0, 1), (1, 0)])

    queries, token = lax.optimization_barrier((queries, stage(queries)))
    turn = {1: 2, 2: 1} if half > 3 else {}
    ways = [(turn.get(k, k), k) for k in range(1, half - 1)]
    early = [
        send(queries, lambda g, e, t, _: (g, e ^ way[1 - (t ^ odd(e))], t)) for way in ways
    ]
    last = []
    far = half - 1
    aside = lambda g, e, t: ((g + 1) % groups, e, t) if groups > 1 else (g, e ^ max(far, 1), t)
    if far:
        last = [
            send(queries, lambda g, e, t, on: (g, e ^ far, t) if on else aside(g, e, t)),
            send(queries, lambda g, e, t, on: (g, e if on else e ^ far, 1 - t)),
        ]

    def whole(steps, *values):
        empty = lambda *_: jax.tree.map(lambda s: jnp.zeros(s.shape, s.dtype), shapes)
        shapes = jax.eval_shape(steps, *values)
        return lax.cond(lax.axis_index("ex") < ex, steps, empty, *values)

    def gradient(part, high, low):
        grad = outer(part, swap(part))
        half_precond = precondition(grad, high, low)
        return grad, both_halves(half_precond, swap(half_precond))

    out_part = project_out(token, out_grads[0], out_factor)
    part, own = project_in(out_part, activations[0].T, in_factor, queries)
    high, low = prepare(curvature_inv)
    grad, precond = gradient(part, high, low)
    blocks = [own, *early]
    far_row = send(precond, lambda g, e, t, on: (g, e, 1 - t) if on else (g, e ^ half, t))
    others = whole(lambda *values: keep(swap(stack(values))), *blocks)
    scores = score(half, [(0, 0), *ways], (precond, far_row), blocks, others)
    if last:
        way = half - 1
        scores = score(half, [(way, way)], (), last[:1], last[1], scores)
    near, far = scores[:2]
    returned = send(far, lambda g, e, t, on: (g, e ^ half, t) if on else (g, e, 1 - t))
    return finish(half, grad, near, returned)


def solution(mesh):
    placed = (
        P(("groups", "ex"), None, "tp"),
        P(("groups", "ex"), None, "tp"),
        P(None, "tp"),
        P(None, "tp"),
        P("tp", None),
        P(("groups", "ex"), "tp"),
    )
    return jax.shard_map(
        functools.partial(shards, (mesh.shape["groups"], mesh.shape["ex"])),
        mesh=mesh,
        in_specs=placed,
        out_specs=(P(("groups", "ex"), "tp"), P(("groups", "ex"), "tp")),
        check_vma=False,
    )
```
